32 devices in a mesh: date: 8 (over z, core), book: 4 (over y, x).
Axes of the slice: x: 2, y: 2, z: 4, core: 2. Of those that a mesh axis runs over, the one named last changes fastest.
Arguments:
- shocks: bfloat16 [16, 512, 2048], P('date', None, 'book'), may hold values from -6 to 6
- persistence: float32 [2048], P('book'), may hold values from 0.5 to 1
- volatility: float32 [2048], P('book'), may hold values from 0.05 to 0.4
- base_rate: float32 [2048], P('book'), may hold values from 0 to 1
- cashflows: bfloat16 [16384, 512], P('book'), may hold values from -0.125 to 0.125
- block_owner: int32 [64, 1], P('book'), may hold values from 0 to 3; in each aligned block of 16 rows (0 to 15, 16 to 31, ...) at most 8 rows name the same one
- trade_set: int32 [16384], P('book'), may hold values from 0 to 511
- threshold: float32 [512], P('book'), may hold values from 0.1 to 1
- margin_lag: int32 [512], P('book'), may hold values from 1 to 2
Outputs:
- net_value: float32 [16, 512, 512], P('date', None, 'book')
- expected_exposure: float32 [16, 512], P('date', 'book')
The draws below stay inside these ranges and needn't reach their ends.
Inputs may be any that keep to these rules, and one draw needn't show every extreme that they name: `block_owner`: among the blocks of one index of book, no value is named by more than 8 blocks.
All inputs are finite; a program needn't handle non-finite values.
Results may differ from the reference program's by a relative error of at most 0.0039.
Values may be sent and summed in bfloat16 or wider, within the bound.
No kernel may reach another device: no remote copies, remote signals or barrier semaphores. Data moves between devices by JAX's collectives and lax.ppermute only.
A program may use at most 128 MiB of HBM per device.

```python
import math
import jax
import jax.numpy as jnp
import numpy as np
from jax import lax

CF = 512
SETS = 512
TB = 256
DATE_DEV = 2
PATHS = 512
BLK_DEV = 16
MOST = 8
DATES = 16
BUCKETS = 2048
BLOCKS = 64
TRADES = 16384
N_BOOK = 4


def touch_ends(array, own_key, least, largest):
    shape = array.shape
    index_at = [jax.random.randint(jax.random.fold_in(own_key, axis), (), 0, shape[axis]) for axis in range(len(shape))]
    array = array.at[tuple(index_at)].set(least)
    longest = shape.index(max(shape))
    index_at[longest] = (index_at[longest] + 1) % shape[longest]
    return array.at[tuple(index_at)].set(largest)


def level_of(rng, shape, shards, least, top_value):
    factor_of = 1.0
    for dim, parts in shards:
        heights = jax.random.uniform(jax.random.fold_in(jax.random.fold_in(rng, 6), dim), (parts,), jnp.float32, least / len(shards), top_value / len(shards))
        factor_of = factor_of * jnp.repeat(jnp.exp(heights), shape[dim] // parts).reshape((-1,) + (1,) * (len(shape) - 1 - dim))
    return factor_of


def assign_block(rng, own, number, rows, number_of, top, limit, slope):
    order = jax.random.permutation(rng, number_of)
    crowded, common = shares(number_of, rows * top, limit, slope, True), shares(number_of, rows * top, limit, slope, False)
    places = jnp.arange(number_of)

    def named(lengths, turn):
        used = int((lengths > 0).sum())
        fixed = max(1, used // 4)
        passed = fixed + (places - fixed + turn * (used - fixed)) % max(1, number_of - fixed)
        return jnp.zeros((number_of,), jnp.int32).at[order[jnp.where(places < fixed, places, passed)]].set(jnp.asarray(lengths, jnp.int32))

    lengths = jnp.where(number % 4 == 0, named(crowded, number // 4), named(common, number - number // 4 - 1))
    mixed = jax.random.permutation(jax.random.fold_in(own, 3), number_of)
    giver, taker = mixed[0:number_of // 2 * 2:2], mixed[1:number_of // 2 * 2:2]
    margin = jnp.minimum(lengths[giver] - 1, limit - lengths[taker]) // 2
    margin = jnp.where((giver == order[0]) | (taker == order[0]) | (lengths[taker] == 0), 0, jnp.maximum(margin, 0))
    passed = jax.random.randint(jax.random.fold_in(own, 4), (number_of // 2,), 0, 1 << 20) % (margin + 1)
    lengths = lengths.at[giver].add(-passed).at[taker].add(passed)
    items = jnp.searchsorted(jnp.cumsum(lengths), jnp.arange(rows * top), side="right").astype(jnp.int32)
    listing = items.reshape(top, rows).T
    listing = listing[jax.random.permutation(jax.random.fold_in(own, 1), rows)]
    turn = jax.random.randint(jax.random.fold_in(own, 2), (rows, 1), 0, top)
    return jnp.take_along_axis(listing, (jnp.arange(top)[None, :] + turn) % top, axis=1)


def shares(count, total, most, slope, full):
    portions = [(1 << 20) // math.isqrt(standing ** slope) + 1 for standing in range(1, count + 1)]
    largest = most if full else min(most, max(-(-total // count), total * portions[0] // sum(portions)))
    least = 1 if total - largest >= count - 1 else 0
    counts, spare = [largest] + [least] * (count - 1), total - largest - least * (count - 1)
    while spare > 0:
        free = [i for i in range(1, count) if counts[i] < largest] or [i for i in range(1, count) if counts[i] < most]
        whole, budget = sum([portions[i] for i in free]), spare
        for i in free:
            extra = min(most - counts[i], max(1, budget * portions[i] // whole), spare)
            counts[i] = counts[i] + extra
            spare = spare - extra
    return np.array(counts)


def scatter_about(stream_key, dims, width, bound, shards=(), held_as=jnp.bfloat16):
    drawn = jax.random.normal(stream_key, dims, jnp.float32) * width
    if len(shards) > 0:
        drawn = level_of(stream_key, dims, shards, -0.22, 0.18) * drawn
    return jnp.clip(drawn, min=-bound, max=bound).astype(held_as)


def setup_inputs(seed: int = 0) -> dict:
    key_list = jax.random.split(jax.random.key(seed), 10)
    shocks = scatter_about(key_list[0], (DATES, PATHS, BUCKETS), 1.0, 6.0, ((0, 8), (2, 4)))
    persistence = jnp.clip(0.5 + 0.5 * jax.random.uniform(key_list[1], (BUCKETS,), jnp.float32) ** level_of(key_list[1], (BUCKETS,), ((0, 4),), -0.2, 0.2), 0.5, 1.0)
    volatility = jnp.clip(jnp.exp(math.log(0.4) - 2.0794415 * jax.random.uniform(key_list[2], (BUCKETS,), jnp.float32) ** level_of(key_list[2], (BUCKETS,), ((0, 4),), -0.2, 0.2)), 0.05, 0.4)
    base_rate = jnp.clip(1.0 * jax.random.uniform(key_list[3], (BUCKETS,), jnp.float32) ** level_of(key_list[3], (BUCKETS,), ((0, 4),), -0.2, 0.2), 0.0, 1.0)
    cashflows = scatter_about(key_list[4], (TRADES, CF), (2.0 * (CF * TRADES // SETS) ** -0.5), 0.125, ((0, 4),))
    block_owner_keys = jax.random.split(jax.random.fold_in(key_list[5], 1), BLOCKS // BLK_DEV)
    block_owner_turns = jax.random.permutation(jax.random.fold_in(key_list[5], 3), BLOCKS // BLK_DEV)
    block_owner = jax.vmap(lambda own, number: assign_block(jax.random.fold_in(key_list[5], 2), own, number, BLK_DEV, N_BOOK, 1, MOST, 2))(block_owner_keys, block_owner_turns).reshape((BLOCKS, 1))
    trade_set = touch_ends(jax.random.randint(key_list[6], (TRADES,), 0, SETS), jax.random.fold_in(key_list[6], 1), 0, SETS - 1).astype(jnp.int32)
    threshold = jnp.clip(jnp.exp(math.log(1.0) - 2.3025851 * jax.random.uniform(key_list[7], (SETS,), jnp.float32) ** level_of(key_list[7], (SETS,), ((0, 4),), -0.2, 0.2)), 0.1, 1.0)
    margin_lag = touch_ends(jax.random.randint(key_list[8], (SETS,), 1, DATE_DEV + 1), jax.random.fold_in(key_list[8], 1), 1, DATE_DEV).astype(jnp.int32)
    return {"shocks": shocks, "persistence": persistence, "volatility": volatility, "base_rate": base_rate, "cashflows": cashflows, "block_owner": block_owner, "trade_set": trade_set, "threshold": threshold, "margin_lag": margin_lag}


def reference(shocks, persistence, volatility, base_rate, cashflows, block_owner, trade_set, threshold, margin_lag):
    def advance(state, shock):
        state = persistence * state + volatility * shock.astype(jnp.float32)
        return state, state

    start = jnp.zeros((PATHS, BUCKETS), jnp.float32)
    _, level = lax.scan(advance, start, shocks)
    discount = jnp.exp(-(base_rate + level)).astype(jnp.bfloat16)
    flat = discount.reshape(DATES * PATHS, BUCKETS)
    owners = block_owner[:, 0].astype(jnp.int32)
    cf_blocks = cashflows.reshape(BLOCKS, TB, CF)
    set_blocks = trade_set.reshape(BLOCKS, TB)
    labels = jnp.arange(SETS, dtype=jnp.int32)

    def add_block(total, item):
        owner, flows, sets = item
        slab = lax.dynamic_slice_in_dim(flat, (owner * CF).astype(jnp.int32), CF, 1)
        price = jnp.dot(slab, flows.T, preferred_element_type=jnp.float32).astype(jnp.bfloat16)
        onehot = (sets[:, None] == labels[None, :]).astype(jnp.bfloat16)
        return total + jnp.dot(price, onehot, preferred_element_type=jnp.float32), None

    total = jnp.zeros((DATES * PATHS, SETS), jnp.float32)
    total, _ = lax.scan(add_block, total, (owners, cf_blocks, set_blocks))
    net_value = total.reshape(DATES, PATHS, SETS)
    collateral = jnp.zeros_like(net_value)
    for lag in range(1, DATE_DEV + 1):
        moved = jnp.concatenate([jnp.zeros((lag, PATHS, SETS), jnp.float32), net_value[:DATES - lag]], 0)
        collateral = jnp.where(margin_lag[None, None, :] == lag, moved, collateral)
    exposure = jnp.maximum(net_value - collateral - threshold[None, None, :], 0.0)
    return net_value, jnp.mean(exposure, axis=1)
```

```python
import functools

import jax
import jax.numpy as jnp
from jax import lax
from jax.experimental import pallas as pl
from jax.experimental.pallas import tpu as pltpu
from jax.sharding import PartitionSpec as P

SETS = 512
CORES = 2
SHOCK = 6.0
TOP = 32760.0
MIB = 1 << 20


def swap(block):
    n = lax.axis_size("date")
    return lax.ppermute(block, "date", [(i, i ^ 1) for i in range(n)])


def later(block, chips):
    n = lax.axis_size("date")
    hop = CORES * chips
    return lax.ppermute(block, "date", [(i, i + hop) for i in range(n - hop)])


def exchange(slots):
    n = len(slots)
    return [
        lax.ppermute(slots[i], "book", [(j, j ^ i) for j in range(n)])
        for i in range(1, n)
    ]


def weights_kernel(books, per, here_ref, owner_ref, sets_ref, flows_ref, *refs):
    outs, total = refs[:books], refs[books]
    step = pl.program_id(0)
    core, me = here_ref[0], here_ref[1]
    half = outs[0].shape[0]
    rows = sets_ref.shape[2] // per
    sets_here = SETS // books

    @pl.when(step == 0)
    def _():
        total[...] = jnp.zeros_like(total)

    row = lax.broadcasted_iota(jnp.int32, (half, rows), 0) + core * half
    for b in range(per):
        owner = owner_ref[step * per + b]
        name = sets_ref[0, :, b * rows : (b + 1) * rows]
        name = ((name // sets_here) ^ owner) * sets_here + name % sets_here
        hot = jnp.where(name == row, 1.0, 0.0).astype(jnp.bfloat16)
        part = jnp.dot(
            hot, flows_ref[b * rows : (b + 1) * rows, :], preferred_element_type=jnp.float32
        )
        slot = owner ^ me
        total[slot] = total[slot] + part

    @pl.when(step == pl.num_programs(0) - 1)
    def _():
        for i in range(books):
            outs[i][...] = total[i].astype(outs[i].dtype)


def weights(here, owners, trade_set, cashflows, books):
    blocks = owners.shape[0]
    trades, width = cashflows.shape
    rows = trades // blocks
    per = 4 if blocks % 4 == 0 else 1
    steps = blocks // per
    half = SETS // CORES
    return pl.pallas_call(
        functools.partial(weights_kernel, books, per),
        grid_spec=pltpu.PrefetchScalarGridSpec(
            num_scalar_prefetch=2,
            grid=(steps,),
            in_specs=[
                pl.BlockSpec((1, 1, per * rows), lambda i, *_: (i, 0, 0)),
                pl.BlockSpec((per * rows, width), lambda i, *_: (i, 0)),
            ],
            out_specs=[pl.BlockSpec((half, width), lambda i, *_: (0, 0))] * books,
            scratch_shapes=[pltpu.VMEM((books, half, width), jnp.float32)],
        ),
        out_shape=[
            jax.ShapeDtypeStruct((half, width), jnp.bfloat16 if i else jnp.float32)
            for i in range(books)
        ],
        compiler_params=pltpu.CompilerParams(vmem_limit_bytes=32 * MIB),
        cost_estimate=pl.CostEstimate(
            flops=2 * trades * half * width, bytes_accessed=2 * trades * width, transcendentals=0
        ),
        name="weights",
    )(here, owners, trade_set.reshape(steps, 1, per * rows), cashflows)


def values_kernel(books, here_ref, par_ref, first_ref, second_ref, start_ref, mine_ref, other_ref, *refs):
    outs, matrix, disc = refs[:books], refs[books], refs[books + 1]
    core = here_ref[0]
    dates, paths, width = first_ref.shape
    half = mine_ref.shape[0]
    matrix[pl.ds(core * half, half), :] = mine_ref[...]
    matrix[pl.ds((1 - core) * half, half), :] = other_ref[...]
    tile = 32

    def walk(i, _):
        at = pl.ds(i * tile, tile)
        pers, vol, base = par_ref[0:1, :], par_ref[1:2, :], par_ref[2:3, :]
        state = start_ref[at, :]
        for t in range(2 * dates):
            source = first_ref if t < dates else second_ref
            state = pers * state + vol * source[t % dates, at, :].astype(jnp.float32)
            disc[pl.ds(t * paths + i * tile, tile), :] = jnp.exp(-(base + state)).astype(jnp.bfloat16)
        return 0

    lax.fori_loop(0, paths // tile, walk, 0)
    sets_here = SETS // books
    rows = 256
    for r in range(2 * dates * paths // rows):
        part = lax.dot_general(
            disc[r * rows : (r + 1) * rows, :],
            matrix[...],
            (((1,), (1,)), ((), ())),
            preferred_element_type=jnp.float32,
        )
        for i in range(books):
            outs[i][r * rows : (r + 1) * rows, :] = part[:, i * sets_here : (i + 1) * sets_here].astype(
                outs[i].dtype
            )


def values(here, par, first, second, start, mine, other, books):
    dates, paths, width = first.shape
    rows = 2 * dates * paths
    whole = pl.BlockSpec(memory_space=pltpu.VMEM)
    return pl.pallas_call(
        functools.partial(values_kernel, books),
        in_specs=[pl.BlockSpec(memory_space=pltpu.SMEM)] + [whole] * 6,
        out_specs=[whole] * books,
        out_shape=[
            jax.ShapeDtypeStruct((rows, SETS // books), jnp.bfloat16 if i else jnp.float32)
            for i in range(books)
        ],
        scratch_shapes=[
            pltpu.VMEM((SETS, width), jnp.bfloat16),
            pltpu.VMEM((rows, width), jnp.bfloat16),
        ],
        compiler_params=pltpu.CompilerParams(vmem_limit_bytes=32 * MIB),
        cost_estimate=pl.CostEstimate(
            flops=2 * rows * SETS * width, bytes_accessed=4 * MIB, transcendentals=rows * width
        ),
        name="values",
    )(here, par, first, second, start, mine, other)


def on_device(
    shocks,
    persistence,
    volatility,
    base_rate,
    cashflows,
    block_owner,
    trade_set,
    threshold,
    margin_lag,
):
    dates, paths, width = shocks.shape
    books = lax.axis_size("book")
    chips = lax.axis_size("date") // CORES
    me = lax.axis_index("book")
    core = lax.axis_index("date") % CORES
    here = jnp.stack([core, me]).astype(jnp.int32)
    half = paths // CORES
    span = CORES * dates

    def side(array, which, axis):
        size = array.shape[axis] // CORES
        return lax.dynamic_slice_in_dim(array, which * size, size, axis)

    kept = side(shocks, core, 1)
    got = swap(side(shocks, 1 - core, 1))
    first = jnp.where(core == 0, kept, got)
    second = jnp.where(core == 0, got, kept)

    power = [jnp.ones_like(persistence)]
    for _ in range(span * chips):
        power.append(power[-1] * persistence)
    decay = power[span]

    gain = jnp.zeros((half, width), jnp.float32)
    for t in range(span):
        source = first if t < dates else second
        gain = persistence * gain + volatility * source[t % dates].astype(jnp.float32)

    mats = weights(here, block_owner[:, 0], trade_set, cashflows, books)

    start = jnp.zeros((half, width), jnp.float32)
    reach, fade = 1, jnp.ones_like(decay)
    while reach < chips:
        bound = SHOCK * volatility * sum(power[: min(reach, chips) * span])
        upto = gain + decay * start
        code = jnp.round(upto * (TOP / bound)).astype(jnp.int16)
        came = later(code, reach).astype(jnp.float32) * (bound / TOP)
        start = start + fade * came
        fade = fade * power[reach * span]
        reach *= 2

    mine = mats[0]
    for part in exchange(mats):
        mine = mine + part.astype(jnp.float32)
    mine = mine.astype(jnp.bfloat16)
    other = swap(mine)

    par = jnp.stack([persistence, volatility, base_rate])
    pieces = values(here, par, first, second, start, mine, other, books)
    net = pieces[0]
    for part in exchange(pieces):
        net = net + part.astype(jnp.float32)
    sets_here = SETS // books
    net = net.reshape(span, half, sets_here)

    before = later(net[span - dates :].astype(jnp.bfloat16), 1).astype(jnp.float32)
    net_got = swap(side(net, 1 - core, 0))
    net_kept = side(net, core, 0)
    net_value = jnp.concatenate(
        [jnp.where(core == 0, net_kept, net_got), jnp.where(core == 0, net_got, net_kept)], 1
    )

    joined = jnp.concatenate([before, net], 0)
    collateral = jnp.zeros_like(net)
    for lag in range(1, dates + 1):
        collateral = jnp.where(
            margin_lag[None, None, :] == lag, joined[dates - lag : dates - lag + span], collateral
        )
    exposure = jnp.sum(jnp.maximum(net - collateral - threshold[None, None, :], 0.0), axis=1)
    exposure = side(exposure, core, 0) + swap(side(exposure, 1 - core, 0))
    return (net_value, exposure / paths)


def solution(mesh):
    return jax.shard_map(
        on_device,
        mesh=mesh,
        in_specs=(
            P("date", None, "book"),
            P("book"),
            P("book"),
            P("book"),
            P("book", None),
            P("book", None),
            P("book"),
            P("book"),
            P("book"),
        ),
        out_specs=(P("date", None, "book"), P("date", "book")),
        check_vma=False,
    )
```

```python
import functools

import jax
import jax.numpy as jnp
from jax import lax
from jax.experimental import pallas as pl
from jax.experimental.pallas import tpu as pltpu
from jax.sharding import PartitionSpec as P

SETS = 512
CORES = 2
SHOCK = 6.0
TOP = 32760.0
CHUNKS = 2
MIB = 1 << 20


def swap(block):
    n = lax.axis_size("date")
    return lax.ppermute(block, "date", [(i, i ^ 1) for i in range(n)])


def later(block, chips):
    n = lax.axis_size("date")
    hop = CORES * chips
    return lax.ppermute(block, "date", [(i, i + hop) for i in range(n - hop)])


def exchange(slots):
    n = len(slots)
    return [
        lax.ppermute(slots[i], "book", [(j, j ^ i) for j in range(n)])
        for i in range(1, n)
    ]


def weights_kernel(books, per, here_ref, owner_ref, sets_ref, flows_ref, *refs):
    outs, total = refs[:books], refs[books]
    step = pl.program_id(0)
    core, me = here_ref[0], here_ref[1]
    half = outs[0].shape[0]
    rows = sets_ref.shape[2] // per
    sets_here = SETS // books

    @pl.when(step == 0)
    def _():
        total[...] = jnp.zeros_like(total)

    row = lax.broadcasted_iota(jnp.int32, (half, rows), 0) + core * half
    for b in range(per):
        owner = owner_ref[step * per + b]
        name = sets_ref[0, :, b * rows : (b + 1) * rows]
        name = ((name // sets_here) ^ owner) * sets_here + name % sets_here
        hot = jnp.where(name == row, 1.0, 0.0).astype(jnp.bfloat16)
        part = jnp.dot(
            hot, flows_ref[b * rows : (b + 1) * rows, :], preferred_element_type=jnp.float32
        )
        slot = owner ^ me
        total[slot] = total[slot] + part

    @pl.when(step == pl.num_programs(0) - 1)
    def _():
        for i in range(books):
            outs[i][...] = total[i].astype(outs[i].dtype)


def weights(here, owners, trade_set, cashflows, books):
    blocks = owners.shape[0]
    trades, width = cashflows.shape
    rows = trades // blocks
    per = 4 if blocks % 4 == 0 else 1
    steps = blocks // per
    half = SETS // CORES
    return pl.pallas_call(
        functools.partial(weights_kernel, books, per),
        grid_spec=pltpu.PrefetchScalarGridSpec(
            num_scalar_prefetch=2,
            grid=(steps,),
            in_specs=[
                pl.BlockSpec((1, 1, per * rows), lambda i, *_: (i, 0, 0)),
                pl.BlockSpec((per * rows, width), lambda i, *_: (i, 0)),
            ],
            out_specs=[pl.BlockSpec((half, width), lambda i, *_: (0, 0))] * books,
            scratch_shapes=[pltpu.VMEM((books, half, width), jnp.float32)],
        ),
        out_shape=[
            jax.ShapeDtypeStruct((half, width), jnp.bfloat16 if i else jnp.float32)
            for i in range(books)
        ],
        compiler_params=pltpu.CompilerParams(vmem_limit_bytes=32 * MIB),
        cost_estimate=pl.CostEstimate(
            flops=2 * trades * half * width, bytes_accessed=2 * trades * width, transcendentals=0
        ),
        name="weights",
    )(here, owners, trade_set.reshape(steps, 1, per * rows), cashflows)


def matrix_kernel(here_ref, mine_ref, other_ref, high_ref, low_ref):
    core = here_ref[0]
    half = mine_ref.shape[0]
    for source, place in ((mine_ref, core), (other_ref, 1 - core)):
        turned = source[...].T
        high = turned.astype(jnp.bfloat16)
        at = pl.ds(pl.multiple_of(place * half, half), half)
        high_ref[:, at] = high
        low_ref[:, at] = (turned - high.astype(jnp.float32)).astype(jnp.bfloat16)


def matrix(here, mine, other):
    half, width = mine.shape
    whole = pl.BlockSpec(memory_space=pltpu.VMEM)
    return pl.pallas_call(
        matrix_kernel,
        in_specs=[pl.BlockSpec(memory_space=pltpu.SMEM)] + [whole] * 2,
        out_specs=[whole] * 2,
        out_shape=[jax.ShapeDtypeStruct((width, CORES * half), jnp.bfloat16)] * 2,
        compiler_params=pltpu.CompilerParams(vmem_limit_bytes=16 * MIB),
        name="matrix",
    )(here, mine, other)


def values_kernel(books, chunk, here_ref, par_ref, kept_ref, got_ref, high_ref, low_ref, *refs):
    codes, outs, disc = refs[: -books - 1], refs[-books - 1 : -1], refs[-1]
    core = here_ref[0]
    dates = kept_ref.shape[0]
    paths = disc.shape[0] // (2 * dates)
    tile = 32

    def walk(i, _):
        at = pl.ds(i * tile, tile)
        from_ = pl.ds(chunk * paths + i * tile, tile)
        pers, vol, base = par_ref[0:1, :], par_ref[1:2, :], par_ref[2:3, :]
        state = jnp.zeros((tile, par_ref.shape[1]), jnp.float32)
        for r, code in enumerate(codes):
            state = state + par_ref[3 + r : 4 + r, :] * code[at, :].astype(jnp.float32)
        for t in range(2 * dates):
            kept = kept_ref[t % dates, from_, :].astype(jnp.float32)
            got = got_ref[t % dates, from_, :].astype(jnp.float32)
            early, late = (kept, got) if t < dates else (got, kept)
            state = pers * state + vol * jnp.where(core == 0, early, late)
            disc[pl.ds(t * paths + i * tile, tile), :] = jnp.exp(-(base + state)).astype(jnp.bfloat16)
        return 0

    lax.fori_loop(0, paths // tile, walk, 0)
    sets_here = SETS // books
    rows = 256
    for r in range(2 * dates * paths // rows):
        price = disc[r * rows : (r + 1) * rows, :]
        part = jnp.dot(price, high_ref[...], preferred_element_type=jnp.float32)
        part = part + jnp.dot(price, low_ref[...], preferred_element_type=jnp.float32)
        for i in range(books):
            outs[i][r * rows : (r + 1) * rows, :] = part[:, i * sets_here : (i + 1) * sets_here].astype(
                outs[i].dtype
            )


def values(here, par, kept, got, high, low, codes, part, books, chunk):
    dates, _, width = kept.shape
    rows = 2 * dates * part
    whole = pl.BlockSpec(memory_space=pltpu.VMEM)
    return pl.pallas_call(
        functools.partial(values_kernel, books, chunk),
        in_specs=[pl.BlockSpec(memory_space=pltpu.SMEM)] + [whole] * (5 + len(codes)),
        out_specs=[whole] * books,
        out_shape=[
            jax.ShapeDtypeStruct((rows, SETS // books), jnp.bfloat16 if i else jnp.float32)
            for i in range(books)
        ],
        scratch_shapes=[pltpu.VMEM((rows, width), jnp.bfloat16)],
        compiler_params=pltpu.CompilerParams(vmem_limit_bytes=16 * MIB),
        cost_estimate=pl.CostEstimate(
            flops=4 * rows * SETS * width, bytes_accessed=2 * MIB, transcendentals=rows * width
        ),
        name="values",
    )(here, par, kept, got, high, low, *codes)


def after(array, *others):
    return lax.optimization_barrier((array,) + others)[0]


def on_device(
    shocks,
    persistence,
    volatility,
    base_rate,
    cashflows,
    block_owner,
    trade_set,
    threshold,
    margin_lag,
):
    dates, paths, width = shocks.shape
    books = lax.axis_size("book")
    chips = lax.axis_size("date") // CORES
    me = lax.axis_index("book")
    core = lax.axis_index("date") % CORES
    here = jnp.stack([core, me]).astype(jnp.int32)
    half = paths // CORES
    span = CORES * dates
    part = half // CHUNKS
    sets_here = SETS // books

    def side(array, which, axis):
        size = array.shape[axis] // CORES
        return lax.dynamic_slice_in_dim(array, which * size, size, axis)

    sent = side(shocks, 1 - core, 1)
    got = swap(sent)
    mats = weights(after(here, sent), block_owner[:, 0], trade_set, cashflows, books)
    mats_arrived = exchange(mats)
    kept = side(after(shocks, mats[0]), core, 1)

    power = [jnp.ones_like(persistence)]
    for _ in range(span * chips):
        power.append(power[-1] * persistence)
    decay = power[span]
    weigh_kept = jnp.where(core == 0, power[dates], power[0])
    weigh_got = jnp.where(core == 0, power[0], power[dates])

    def own_sum(array):
        total = array[0].astype(jnp.float32)
        for t in range(1, dates):
            total = persistence * total + array[t].astype(jnp.float32)
        return total

    def gain(c):
        rows = slice(c * part, (c + 1) * part)
        return volatility * (weigh_kept * own_sum(kept[:, rows]) + weigh_got * own_sum(got[:, rows]))

    codes = [[] for _ in range(CHUNKS)]
    rates = []
    reach, fade = 1, jnp.ones_like(decay)
    last = mats[0]
    while reach < chips:
        bound = SHOCK * volatility * sum(power[: min(reach, chips) * span])
        for c in range(CHUNKS):
            upto = gain(c)
            for i in range(len(codes[c])):
                came = after(codes[c][i], last)
                upto = upto + (decay * rates[i]) * came.astype(jnp.float32)
            if not codes[c]:
                upto = after(upto, last)
            code = jnp.round(upto * (TOP / bound)).astype(jnp.int16)
            last = code
            codes[c].append(later(code, reach))
        rates.append(fade * (bound / TOP))
        fade = fade * power[reach * span]
        reach *= 2

    mine = after(mats[0], last, *codes[0])
    for arrived in mats_arrived:
        mine = mine + arrived.astype(jnp.float32)
    high, low = matrix(here, mine, swap(mine))

    par = jnp.stack([persistence, volatility, base_rate] + rates)
    pieces, arrivals = [], []
    last = high
    for c in range(CHUNKS):
        came = [after(code, last) for code in codes[c]]
        pieces.append(values(here, par, kept, got, high, low, came, part, books, c))
        arrivals.append(exchange(pieces[c]))
        last = pieces[c][0]

    kept_out, got_out, exposed = [], [], jnp.zeros((span, sets_here), jnp.float32)
    for c in range(CHUNKS):
        net = after(pieces[c][0], last)
        for arrived in arrivals[c]:
            net = net + arrived.astype(jnp.float32)
        net = net.reshape(span, part, sets_here)
        before = later(net[span - dates :].astype(jnp.bfloat16), 1).astype(jnp.float32)
        got_out.append(swap(side(net, 1 - core, 0)))
        kept_out.append(side(net, core, 0))
        joined = jnp.concatenate([before, net], 0)
        collateral = jnp.zeros_like(net)
        for lag in range(1, dates + 1):
            collateral = jnp.where(
                margin_lag[None, None, :] == lag, joined[dates - lag : dates - lag + span], collateral
            )
        exposed = exposed + jnp.sum(jnp.maximum(net - collateral - threshold[None, None, :], 0.0), axis=1)
        last = exposed

    exposed_got = swap(side(exposed, 1 - core, 0))
    kept_out[0] = after(kept_out[0], exposed)
    low_half = [jnp.where(core == 0, a, b) for a, b in zip(kept_out, got_out)]
    high_half = [jnp.where(core == 0, b, a) for a, b in zip(kept_out, got_out)]
    net_value = jnp.concatenate(low_half + high_half, 1)
    net_value, exposed_got = lax.optimization_barrier((net_value, exposed_got))
    return (net_value, (side(exposed, core, 0) + exposed_got) / paths)


def solution(mesh):
    return jax.shard_map(
        on_device,
        mesh=mesh,
        in_specs=(
            P("date", None, "book"),
            P("book"),
            P("book"),
            P("book"),
            P("book", None),
            P("book", None),
            P("book"),
            P("book"),
            P("book"),
        ),
        out_specs=(P("date", None, "book"), P("date", "book")),
        check_vma=False,
    )
```

```python
import functools

import jax
import jax.numpy as jnp
from jax import lax
from jax.experimental import pallas as pl
from jax.experimental.pallas import tpu as pltpu
from jax.sharding import PartitionSpec as P

SETS = 512
CORES = 2
SHOCK = 6.0
TOP = 32760.0
MIB = 1 << 20
TURNED = (((1,), (1,)), ((), ()))


def swap(block):
    n = lax.axis_size("date")
    return lax.ppermute(block, "date", [(i, i ^ 1) for i in range(n)])


def across(block, chips):
    n = lax.axis_size("date")
    hop = CORES * chips
    return lax.ppermute(block, "date", [(i, i ^ hop) for i in range(n)])


def later(block):
    n = lax.axis_size("date")
    return lax.ppermute(block, "date", [(i, i + CORES) for i in range(n - CORES)])


def exchange(slots):
    n = len(slots)
    return [
        lax.ppermute(slots[i], "book", [(j, j ^ i) for j in range(n)])
        for i in range(1, n)
    ]


def weights_kernel(books, per, here_ref, owner_ref, sets_ref, flows_hbm, *refs):
    outs, total, flows, sems = refs[:books], refs[books], refs[books + 1], refs[books + 2]
    core, me = here_ref[0], here_ref[1]
    half = outs[0].shape[0]
    blocks, rows = sets_ref.shape
    sets_here = SETS // books
    size = per * rows
    copies = []
    for step in range(blocks // per):
        at = pl.ds(step * size, size)
        copies.append(pltpu.make_async_copy(flows_hbm.at[at], flows.at[at], sems.at[step]))
        copies[-1].start()
    total[...] = jnp.zeros_like(total)
    row = lax.broadcasted_iota(jnp.int32, (half, rows), 0) + core * half
    for b in range(blocks):
        if b % per == 0:
            copies[b // per].wait()
        owner = owner_ref[b]
        name = sets_ref[b : b + 1, :]
        name = ((name // sets_here) ^ owner) * sets_here + name % sets_here
        hot = jnp.where(name == row, 1.0, 0.0).astype(jnp.bfloat16)
        part = jnp.dot(
            hot, flows[b * rows : (b + 1) * rows, :], preferred_element_type=jnp.float32
        )
        slot = owner ^ me
        total[slot] = total[slot] + part
    for i in range(books):
        outs[i][...] = total[i].astype(outs[i].dtype)


def weights(here, owners, trade_set, cashflows, books):
    blocks = owners.shape[0]
    trades, width = cashflows.shape
    per = 4 if blocks % 4 == 0 else 1
    half = SETS // CORES
    whole = pl.BlockSpec(memory_space=pltpu.VMEM)
    scalars = pl.BlockSpec(memory_space=pltpu.SMEM)
    return pl.pallas_call(
        functools.partial(weights_kernel, books, per),
        in_specs=[scalars, scalars, whole, pl.BlockSpec(memory_space=pltpu.HBM)],
        out_specs=[whole] * books,
        scratch_shapes=[
            pltpu.VMEM((books, half, width), jnp.float32),
            pltpu.VMEM((trades, width), jnp.bfloat16),
            pltpu.SemaphoreType.DMA((blocks // per,)),
        ],
        out_shape=[
            jax.ShapeDtypeStruct((half, width), jnp.bfloat16 if i else jnp.float32)
            for i in range(books)
        ],
        compiler_params=pltpu.CompilerParams(vmem_limit_bytes=24 * MIB),
        cost_estimate=pl.CostEstimate(
            flops=2 * trades * half * width, bytes_accessed=2 * trades * width, transcendentals=0
        ),
        name="weights",
    )(here, owners, trade_set.reshape(blocks, trades // blocks), cashflows)


def price_rows(books, disc, high_ref, low_ref, outs):
    sets_here = SETS // books
    rows = 256
    for r in range(disc.shape[0] // rows):
        price = disc[r * rows : (r + 1) * rows, :]
        part = lax.dot_general(price, high_ref[...], TURNED, preferred_element_type=jnp.float32)
        part = part + lax.dot_general(price, low_ref[...], TURNED, preferred_element_type=jnp.float32)
        for i in range(books):
            outs[i][r * rows : (r + 1) * rows, :] = part[:, i * sets_here : (i + 1) * sets_here].astype(
                outs[i].dtype
            )


def late_kernel(books, here_ref, par_ref, kept_ref, got_ref, start_ref, *refs):
    sources, outs, (early, high, low, late) = refs[:4], refs[4 : 4 + books], refs[4 + books :]
    core = here_ref[0]
    dates, paths, _ = kept_ref.shape
    half = sources[0].shape[0]
    tile = 32
    for i, source in enumerate(sources):
        place = core if i < 2 else 1 - core
        target = low if i % 2 else high
        target[pl.ds(pl.multiple_of(place * half, half), half), :] = source[...]

    def walk(i, _):
        at = pl.ds(i * tile, tile)
        pers, vol, base = par_ref[0:1, :], par_ref[1:2, :], par_ref[2:3, :]
        state = start_ref[at, :]
        for t in range(2 * dates):
            kept = kept_ref[t % dates, at, :].astype(jnp.float32)
            got = got_ref[t % dates, at, :].astype(jnp.float32)
            shock = jnp.where(core == 0, kept, got) if t < dates else jnp.where(core == 0, got, kept)
            state = pers * state + vol * shock
            disc = early if t < dates else late
            disc[pl.ds((t % dates) * paths + i * tile, tile), :] = jnp.exp(-(base + state)).astype(jnp.bfloat16)
        return 0

    lax.fori_loop(0, paths // tile, walk, 0)
    price_rows(books, late, high, low, outs)


def late_values(here, par, kept, got, start, mats, books):
    dates, paths, width = kept.shape
    rows = dates * paths
    whole = pl.BlockSpec(memory_space=pltpu.VMEM)
    *pieces, early, high, low = pl.pallas_call(
        functools.partial(late_kernel, books),
        in_specs=[pl.BlockSpec(memory_space=pltpu.SMEM)] + [whole] * 8,
        out_specs=[whole] * (books + 3),
        out_shape=[
            jax.ShapeDtypeStruct((rows, SETS // books), jnp.bfloat16 if i else jnp.float32)
            for i in range(books)
        ]
        + [jax.ShapeDtypeStruct((rows, width), jnp.bfloat16)]
        + [jax.ShapeDtypeStruct((SETS, width), jnp.bfloat16)] * 2,
        scratch_shapes=[pltpu.VMEM((rows, width), jnp.bfloat16)],
        compiler_params=pltpu.CompilerParams(vmem_limit_bytes=16 * MIB),
        cost_estimate=pl.CostEstimate(
            flops=4 * rows * SETS * width, bytes_accessed=2 * MIB, transcendentals=2 * rows * width
        ),
        name="late_values",
    )(here, par, kept, got, start, *mats)
    return pieces, (early, high, low)


def early_kernel(books, early_ref, high_ref, low_ref, *outs):
    price_rows(books, early_ref, high_ref, low_ref, outs)


def early_values(early, high, low, books):
    rows, width = early.shape
    whole = pl.BlockSpec(memory_space=pltpu.VMEM)
    return pl.pallas_call(
        functools.partial(early_kernel, books),
        in_specs=[whole] * 3,
        out_specs=[whole] * books,
        out_shape=[
            jax.ShapeDtypeStruct((rows, SETS // books), jnp.bfloat16 if i else jnp.float32)
            for i in range(books)
        ],
        compiler_params=pltpu.CompilerParams(vmem_limit_bytes=12 * MIB),
        cost_estimate=pl.CostEstimate(
            flops=4 * rows * SETS * width, bytes_accessed=2 * MIB, transcendentals=0
        ),
        name="early_values",
    )(early, high, low)


def after(array, *others):
    return lax.optimization_barrier((array,) + others)[0]


def on_device(
    shocks,
    persistence,
    volatility,
    base_rate,
    cashflows,
    block_owner,
    trade_set,
    threshold,
    margin_lag,
):
    dates, paths, width = shocks.shape
    books = lax.axis_size("book")
    chips = lax.axis_size("date") // CORES
    me = lax.axis_index("book")
    core = lax.axis_index("date") % CORES
    chip = lax.axis_index("date") // CORES
    here = jnp.stack([core, me]).astype(jnp.int32)
    half = paths // CORES
    span = CORES * dates
    sets_here = SETS // books

    def side(array, which, axis):
        size = array.shape[axis] // CORES
        return lax.dynamic_slice_in_dim(array, which * size, size, axis)

    sent = side(shocks, 1 - core, 1)
    got = swap(sent)
    kept = side(after(shocks, sent), core, 1)

    power = [jnp.ones_like(persistence)]
    for _ in range(span * chips):
        power.append(power[-1] * persistence)

    def own_sum(array):
        total = array[0].astype(jnp.float32)
        for t in range(1, dates):
            total = persistence * total + array[t].astype(jnp.float32)
        return total

    weigh_kept = volatility * jnp.where(core == 0, power[dates], power[0])
    weigh_got = volatility * jnp.where(core == 0, power[0], power[dates])
    group = weigh_kept * own_sum(kept) + weigh_got * own_sum(got)

    codes, rates = [], []
    reach, inside = 1, power[0]
    while reach < chips:
        bound = SHOCK * volatility * sum(power[: reach * span])
        code = jnp.round(group * (TOP / bound)).astype(jnp.int16)
        if reach == 1:
            mats = weights(after(here, code), block_owner[:, 0], trade_set, cashflows, books)
            mats_arrived = exchange(mats)
        came = across(code, reach)
        odd = (chip // reach) % 2 == 1
        fall = power[reach * span]
        rates.append(jnp.where(odd, inside, 0.0) * (bound / TOP))
        codes.append(came)
        came = after(came, mats[0]).astype(jnp.float32) * (bound / TOP)
        group = jnp.where(odd, power[0], fall) * group + jnp.where(odd, fall, power[0]) * came
        inside = inside * jnp.where(odd, fall, power[0])
        reach *= 2

    mine = after(mats[0], code)
    for arrived in mats_arrived:
        mine = mine + arrived.astype(jnp.float32)
    high = mine.astype(jnp.bfloat16)
    low = (mine - high.astype(jnp.float32)).astype(jnp.bfloat16)
    start = jnp.zeros((half, width), jnp.float32)
    for came, rate in zip(codes, rates):
        start = start + rate * came.astype(jnp.float32)

    par = jnp.stack([persistence, volatility, base_rate])
    late_pieces, rest = late_values(here, par, kept, got, start, [high, low, swap(high), swap(low)], books)
    late_arrived = exchange(late_pieces)
    early_pieces = early_values(*rest, books)
    early_arrived = exchange(early_pieces)

    def gathered(piece, others):
        net = piece
        for arrived in others:
            net = net + arrived.astype(jnp.float32)
        return net.reshape(dates, half, sets_here)

    late_net = gathered(after(late_pieces[0], early_pieces[0]), late_arrived)
    before = later(late_net.astype(jnp.bfloat16))
    early_net = gathered(after(early_pieces[0], late_net), early_arrived)
    net_got = swap(jnp.where(core == 0, late_net, early_net))
    net_kept = jnp.where(core == 0, early_net, late_net)

    joined = jnp.concatenate([before.astype(jnp.float32), early_net, late_net], 0)
    now = joined[dates:]
    collateral = jnp.zeros_like(now)
    for lag in range(1, dates + 1):
        collateral = jnp.where(
            margin_lag[None, None, :] == lag, joined[dates - lag : dates - lag + span], collateral
        )
    exposed = jnp.sum(jnp.maximum(now - collateral - threshold[None, None, :], 0.0), axis=1)
    exposed_got = swap(side(exposed, 1 - core, 0))
    net_kept = after(net_kept, exposed)
    net_value = jnp.concatenate(
        [jnp.where(core == 0, net_kept, net_got), jnp.where(core == 0, net_got, net_kept)], 1
    )
    net_value, exposed_got = lax.optimization_barrier((net_value, exposed_got))
    return (net_value, (side(exposed, core, 0) + exposed_got) / paths)


def solution(mesh):
    return jax.shard_map(
        on_device,
        mesh=mesh,
        in_specs=(
            P("date", None, "book"),
            P("book"),
            P("book"),
            P("book"),
            P("book", None),
            P("book", None),
            P("book"),
            P("book"),
            P("book"),
        ),
        out_specs=(P("date", None, "book"), P("date", "book")),
        check_vma=False,
    )
```

```python
import functools

import jax
import jax.numpy as jnp
from jax import lax
from jax.experimental import pallas as pl
from jax.experimental.pallas import tpu as pltpu
from jax.sharding import PartitionSpec as P

SETS = 512
CORES = 2
SHOCK = 6.0
TOP = 32760.0
MIB = 1 << 20
TURNED = (((1,), (1,)), ((), ()))


def swap(block):
    n = lax.axis_size("date")
    return lax.ppermute(block, "date", [(i, i ^ 1) for i in range(n)])


def across(block, chips):
    n = lax.axis_size("date")
    hop = CORES * chips
    return lax.ppermute(block, "date", [(i, i ^ hop) for i in range(n)])


def later(block):
    n = lax.axis_size("date")
    return lax.ppermute(block, "date", [(i, i + CORES) for i in range(n - CORES)])


def exchange(slots):
    n = len(slots)
    return [
        lax.ppermute(slots[i], "book", [(j, j ^ i) for j in range(n)])
        for i in range(1, n)
    ]


def weights_kernel(books, per, here_ref, owner_ref, sets_ref, flows_hbm, *refs):
    outs, total, flows, sems = refs[:books], refs[books], refs[books + 1], refs[books + 2]
    core, me = here_ref[0], here_ref[1]
    half = outs[0].shape[0]
    blocks, rows = sets_ref.shape
    sets_here = SETS // books
    size = per * rows
    copies = []
    for step in range(blocks // per):
        at = pl.ds(step * size, size)
        copies.append(pltpu.make_async_copy(flows_hbm.at[at], flows.at[at], sems.at[step]))
        copies[-1].start()
    total[...] = jnp.zeros_like(total)
    row = lax.broadcasted_iota(jnp.int32, (half, rows), 0) + core * half
    for b in range(blocks):
        if b % per == 0:
            copies[b // per].wait()
        owner = owner_ref[b]
        name = sets_ref[b : b + 1, :]
        name = ((name // sets_here) ^ owner) * sets_here + name % sets_here
        hot = jnp.where(name == row, 1.0, 0.0).astype(jnp.bfloat16)
        part = jnp.dot(
            hot, flows[b * rows : (b + 1) * rows, :], preferred_element_type=jnp.float32
        )
        slot = owner ^ me
        total[slot] = total[slot] + part
    for i in range(books):
        outs[i][...] = total[i].astype(outs[i].dtype)


def weights(here, owners, trade_set, cashflows, books):
    blocks = owners.shape[0]
    trades, width = cashflows.shape
    per = 4 if blocks % 4 == 0 else 1
    half = SETS // CORES
    whole = pl.BlockSpec(memory_space=pltpu.VMEM)
    scalars = pl.BlockSpec(memory_space=pltpu.SMEM)
    return pl.pallas_call(
        functools.partial(weights_kernel, books, per),
        in_specs=[scalars, scalars, whole, pl.BlockSpec(memory_space=pltpu.HBM)],
        out_specs=[whole] * books,
        scratch_shapes=[
            pltpu.VMEM((books, half, width), jnp.float32),
            pltpu.VMEM((trades, width), jnp.bfloat16),
            pltpu.SemaphoreType.DMA((blocks // per,)),
        ],
        out_shape=[
            jax.ShapeDtypeStruct((half, width), jnp.bfloat16 if i else jnp.float32)
            for i in range(books)
        ],
        compiler_params=pltpu.CompilerParams(vmem_limit_bytes=24 * MIB),
        cost_estimate=pl.CostEstimate(
            flops=2 * trades * half * width, bytes_accessed=2 * trades * width, transcendentals=0
        ),
        name="weights",
    )(
        here,
        pltpu.with_memory_space_constraint(owners, pltpu.HBM),
        trade_set.reshape(blocks, trades // blocks),
        pltpu.with_memory_space_constraint(cashflows, pltpu.HBM),
    )


def price_rows(books, disc, high_ref, low_ref, outs):
    sets_here = SETS // books
    rows = 256
    for r in range(disc.shape[0] // rows):
        price = disc[r * rows : (r + 1) * rows, :]
        part = lax.dot_general(price, high_ref[...], TURNED, preferred_element_type=jnp.float32)
        part = part + lax.dot_general(price, low_ref[...], TURNED, preferred_element_type=jnp.float32)
        for i in range(books):
            outs[i][r * rows : (r + 1) * rows, :] = part[:, i * sets_here : (i + 1) * sets_here].astype(
                outs[i].dtype
            )


def values_kernel(books, here_ref, par_ref, kept_ref, got_ref, start_ref, *refs):
    sources, outs, (disc, high, low) = refs[:4], refs[4:-3], refs[-3:]
    core = here_ref[0]
    dates, paths, _ = kept_ref.shape
    half = sources[0].shape[0]
    tile = 32
    for i, source in enumerate(sources):
        place = core if i < 2 else 1 - core
        target = low if i % 2 else high
        target[pl.ds(pl.multiple_of(place * half, half), half), :] = source[...]

    def walk(i, _):
        at = pl.ds(i * tile, tile)
        pers, vol, base = par_ref[0:1, :], par_ref[1:2, :], par_ref[2:3, :]
        state = start_ref[at, :]
        for t in range(2 * dates):
            kept = kept_ref[t % dates, at, :].astype(jnp.float32)
            got = got_ref[t % dates, at, :].astype(jnp.float32)
            shock = jnp.where(core == 0, kept, got) if t < dates else jnp.where(core == 0, got, kept)
            state = pers * state + vol * shock
            disc[pl.ds(t * paths + i * tile, tile), :] = jnp.exp(-(base + state)).astype(jnp.bfloat16)
        return 0

    lax.fori_loop(0, paths // tile, walk, 0)
    rows = dates * paths
    price_rows(books, disc.at[rows:], high, low, outs[:books])
    price_rows(books, disc.at[:rows], high, low, outs[books:])


def values(here, par, kept, got, start, mats, books):
    dates, paths, width = kept.shape
    rows = dates * paths
    whole = pl.BlockSpec(memory_space=pltpu.VMEM)
    pieces = pl.pallas_call(
        functools.partial(values_kernel, books),
        in_specs=[pl.BlockSpec(memory_space=pltpu.SMEM)] + [whole] * 8,
        out_specs=[whole] * (2 * books),
        out_shape=[
            jax.ShapeDtypeStruct((rows, SETS // books), jnp.bfloat16 if i else jnp.float32)
            for i in range(books)
        ]
        * 2,
        scratch_shapes=[pltpu.VMEM((2 * rows, width), jnp.bfloat16)]
        + [pltpu.VMEM((SETS, width), jnp.bfloat16)] * 2,
        compiler_params=pltpu.CompilerParams(vmem_limit_bytes=16 * MIB),
        cost_estimate=pl.CostEstimate(
            flops=8 * rows * SETS * width, bytes_accessed=2 * MIB, transcendentals=2 * rows * width
        ),
        name="values",
    )(here, par, kept, got, start, *mats)
    return pieces[:books], pieces[books:]


def code_kernel(chips, here_ref, par_ref, kept_ref, got_ref, code_ref, group_ref, rows_ref):
    core, chip = here_ref[0], here_ref[2]
    dates, paths, _ = kept_ref.shape
    pers, vol = par_ref[0:1, :], par_ref[1:2, :]
    one = jnp.ones_like(pers)
    span = CORES * dates
    fall, block, reach = one, jnp.zeros_like(pers), 1
    for _ in range(span):
        block = block + fall
        fall = fall * pers
    inside, count = one, 0
    while reach < chips:
        bound = SHOCK * vol * block
        odd = (chip // reach) % 2 == 1
        rows_ref[4 * count : 4 * count + 1, :] = TOP / bound
        rows_ref[4 * count + 1 : 4 * count + 2, :] = jnp.where(odd, inside, 0.0) * (bound / TOP)
        rows_ref[4 * count + 2 : 4 * count + 3, :] = jnp.where(odd, one, fall)
        rows_ref[4 * count + 3 : 4 * count + 4, :] = jnp.where(odd, fall, one) * (bound / TOP)
        inside = inside * jnp.where(odd, fall, one)
        block = block + fall * block
        fall = fall * fall
        reach, count = 2 * reach, count + 1
    tile = 32
    scale = rows_ref[0:1, :]

    def walk(i, _):
        at = pl.ds(i * tile, tile)
        state = jnp.zeros((tile, pers.shape[1]), jnp.float32)
        for t in range(2 * dates):
            kept = kept_ref[t % dates, at, :].astype(jnp.float32)
            got = got_ref[t % dates, at, :].astype(jnp.float32)
            shock = jnp.where(core == 0, kept, got) if t < dates else jnp.where(core == 0, got, kept)
            state = pers * state + vol * shock
        group_ref[at, :] = state
        code_ref[at, :] = jnp.round(state * scale).astype(jnp.int16)
        return 0

    lax.fori_loop(0, paths // tile, walk, 0)


def first_code(here, par, kept, got, chips):
    dates, paths, width = kept.shape
    whole = pl.BlockSpec(memory_space=pltpu.VMEM)
    rounds = max(1, (chips - 1).bit_length())
    return pl.pallas_call(
        functools.partial(code_kernel, chips),
        in_specs=[pl.BlockSpec(memory_space=pltpu.SMEM)] + [whole] * 3,
        out_specs=[whole] * 3,
        out_shape=[
            jax.ShapeDtypeStruct((paths, width), jnp.int16),
            jax.ShapeDtypeStruct((paths, width), jnp.float32),
            jax.ShapeDtypeStruct((4 * rounds, width), jnp.float32),
        ],
        compiler_params=pltpu.CompilerParams(vmem_limit_bytes=8 * MIB),
        cost_estimate=pl.CostEstimate(
            flops=16 * paths * width, bytes_accessed=2 * MIB, transcendentals=0
        ),
        name="first_code",
    )(here, par, kept, got)


def after(array, *others):
    return lax.optimization_barrier((array,) + others)[0]


def on_device(
    shocks,
    persistence,
    volatility,
    base_rate,
    cashflows,
    block_owner,
    trade_set,
    threshold,
    margin_lag,
):
    dates, paths, width = shocks.shape
    books = lax.axis_size("book")
    chips = lax.axis_size("date") // CORES
    me = lax.axis_index("book")
    core = lax.axis_index("date") % CORES
    chip = lax.axis_index("date") // CORES
    here = jnp.stack([core, me, chip]).astype(jnp.int32)
    half = paths // CORES
    span = CORES * dates
    sets_here = SETS // books

    def side(array, which, axis):
        size = array.shape[axis] // CORES
        return lax.dynamic_slice_in_dim(array, which * size, size, axis)

    par = jnp.stack([persistence, volatility, base_rate])
    sent = side(after(shocks, par), 1 - core, 1)
    got = swap(sent)
    kept = side(after(shocks, sent), core, 1)

    code, group, table = first_code(here, par, kept, got, chips)
    start = jnp.zeros((half, width), jnp.float32)
    reach, count = 1, 0
    while reach < chips:
        scale, rate, ours, theirs = (table[4 * count + i] for i in range(4))
        if count:
            code = jnp.round(group * scale).astype(jnp.int16)
        else:
            mats = weights(after(here, code), block_owner[:, 0], trade_set, cashflows, books)
            mats_arrived = exchange(mats)
        came = across(code, reach)
        start = start + rate * came.astype(jnp.float32)
        group = ours * group + theirs * after(came, mats[0]).astype(jnp.float32)
        reach, count = 2 * reach, count + 1

    mine = after(mats[0], code)
    for arrived in mats_arrived:
        mine = mine + arrived.astype(jnp.float32)
    rounded = lax.reduce_precision(mine, 8, 7)
    high, low = rounded.astype(jnp.bfloat16), (mine - rounded).astype(jnp.bfloat16)

    late_pieces, early_pieces = values(
        here, par, kept, got, start, [high, low, swap(high), swap(low)], books
    )
    late_arrived = exchange(late_pieces)
    early_arrived = exchange(early_pieces)

    def gathered(piece, others):
        net = piece
        for arrived in others:
            net = net + arrived.astype(jnp.float32)
        return net.reshape(dates, half, sets_here)

    late_net = gathered(late_pieces[0], late_arrived)
    before = later(late_net.astype(jnp.bfloat16))
    early_net = gathered(after(early_pieces[0], late_net), early_arrived)
    net_got = swap(jnp.where(core == 0, late_net, early_net))
    net_kept = jnp.where(core == 0, early_net, late_net)

    joined = jnp.concatenate([before.astype(jnp.float32), early_net, late_net], 0)
    now = joined[dates:]
    collateral = jnp.zeros_like(now)
    for lag in range(1, dates + 1):
        collateral = jnp.where(
            margin_lag[None, None, :] == lag, joined[dates - lag : dates - lag + span], collateral
        )
    exposed = jnp.sum(jnp.maximum(now - collateral - threshold[None, None, :], 0.0), axis=1)
    exposed_got = swap(side(exposed, 1 - core, 0))
    net_kept = after(net_kept, exposed)
    net_value = jnp.concatenate(
        [jnp.where(core == 0, net_kept, net_got), jnp.where(core == 0, net_got, net_kept)], 1
    )
    net_value, exposed_got = lax.optimization_barrier((net_value, exposed_got))
    return (net_value, (side(exposed, core, 0) + exposed_got) / paths)


def solution(mesh):
    return jax.shard_map(
        on_device,
        mesh=mesh,
        in_specs=(
            P("date", None, "book"),
            P("book"),
            P("book"),
            P("book"),
            P("book", None),
            P("book", None),
            P("book"),
            P("book"),
            P("book"),
        ),
        out_specs=(P("date", None, "book"), P("date", "book")),
        check_vma=False,
    )
```

```python
import functools

import jax
import jax.numpy as jnp
from jax import lax
from jax.experimental import pallas as pl
from jax.experimental.pallas import tpu as pltpu
from jax.sharding import PartitionSpec as P

SETS = 512
CORES = 2
SHOCK = 6.0
TOP = 32760.0
MIB = 1 << 20
TURNED = (((1,), (1,)), ((), ()))


def swap(block):
    n = lax.axis_size("date")
    return lax.ppermute(block, "date", [(i, i ^ 1) for i in range(n)])


def across(block, chips):
    n = lax.axis_size("date")
    hop = CORES * chips
    return lax.ppermute(block, "date", [(i, i ^ hop) for i in range(n)])


def later(block):
    n = lax.axis_size("date")
    return lax.ppermute(block, "date", [(i, i + CORES) for i in range(n - CORES)])


def exchange(slots):
    n = len(slots)
    return [
        lax.ppermute(slots[i], "book", [(j, j ^ i) for j in range(n)])
        for i in range(1, n)
    ]


def weights_kernel(books, per, here_ref, owner_ref, sets_ref, flows_hbm, *refs):
    outs, total, flows, sems = refs[:books], refs[books], refs[books + 1], refs[books + 2]
    core, me = here_ref[0], here_ref[1]
    half = outs[0].shape[0]
    blocks, rows = sets_ref.shape
    sets_here = SETS // books
    size = per * rows
    copies = []
    for step in range(blocks // per):
        at = pl.ds(step * size, size)
        copies.append(pltpu.make_async_copy(flows_hbm.at[at], flows.at[at], sems.at[step]))
        copies[-1].start()
    total[...] = jnp.zeros_like(total)
    row = lax.broadcasted_iota(jnp.int32, (half, rows), 0) + core * half
    for b in range(blocks):
        if b % per == 0:
            copies[b // per].wait()
        owner = owner_ref[b]
        name = sets_ref[b : b + 1, :]
        name = ((name // sets_here) ^ owner) * sets_here + name % sets_here
        hot = jnp.where(name == row, 1.0, 0.0).astype(jnp.bfloat16)
        part = jnp.dot(
            hot, flows[b * rows : (b + 1) * rows, :], preferred_element_type=jnp.float32
        )
        slot = owner ^ me
        total[slot] = total[slot] + part
    for i in range(books):
        outs[i][...] = total[i].astype(outs[i].dtype)


def weights(here, owners, trade_set, cashflows, books):
    blocks = owners.shape[0]
    trades, width = cashflows.shape
    per = 4 if blocks % 4 == 0 else 1
    half = SETS // CORES
    whole = pl.BlockSpec(memory_space=pltpu.VMEM)
    scalars = pl.BlockSpec(memory_space=pltpu.SMEM)
    return pl.pallas_call(
        functools.partial(weights_kernel, books, per),
        in_specs=[scalars, scalars, whole, pl.BlockSpec(memory_space=pltpu.HBM)],
        out_specs=[whole] * books,
        scratch_shapes=[
            pltpu.VMEM((books, half, width), jnp.float32),
            pltpu.VMEM((trades, width), jnp.bfloat16),
            pltpu.SemaphoreType.DMA((blocks // per,)),
        ],
        out_shape=[
            jax.ShapeDtypeStruct((half, width), jnp.bfloat16 if i else jnp.float32)
            for i in range(books)
        ],
        compiler_params=pltpu.CompilerParams(vmem_limit_bytes=24 * MIB),
        cost_estimate=pl.CostEstimate(
            flops=2 * trades * half * width, bytes_accessed=2 * trades * width, transcendentals=0
        ),
        name="weights",
    )(
        here,
        pltpu.with_memory_space_constraint(owners, pltpu.HBM),
        trade_set.reshape(blocks, trades // blocks),
        pltpu.with_memory_space_constraint(cashflows, pltpu.HBM),
    )


def price_rows(books, disc, high_ref, low_ref, outs):
    sets_here = SETS // books
    rows = 256
    for r in range(disc.shape[0] // rows):
        price = disc[r * rows : (r + 1) * rows, :]
        part = lax.dot_general(price, high_ref[...], TURNED, preferred_element_type=jnp.float32)
        part = part + lax.dot_general(price, low_ref[...], TURNED, preferred_element_type=jnp.float32)
        for i in range(books):
            outs[i][r * rows : (r + 1) * rows, :] = part[:, i * sets_here : (i + 1) * sets_here].astype(
                outs[i].dtype
            )


def values_kernel(books, here_ref, par_ref, kept_ref, got_ref, start_ref, *refs):
    sources, outs, (disc, high, low) = refs[:4], refs[4:-3], refs[-3:]
    core = here_ref[0]
    dates, paths, _ = kept_ref.shape
    half = sources[0].shape[0]
    tile = 32
    for i, source in enumerate(sources):
        place = core if i < 2 else 1 - core
        target = low if i % 2 else high
        target[pl.ds(pl.multiple_of(place * half, half), half), :] = source[...]

    def walk(i, _):
        at = pl.ds(i * tile, tile)
        pers, vol, base = par_ref[0:1, :], par_ref[1:2, :], par_ref[2:3, :]
        state = start_ref[at, :]
        for t in range(2 * dates):
            kept = kept_ref[t % dates, at, :].astype(jnp.float32)
            got = got_ref[t % dates, at, :].astype(jnp.float32)
            shock = jnp.where(core == 0, kept, got) if t < dates else jnp.where(core == 0, got, kept)
            state = pers * state + vol * shock
            disc[pl.ds(t * paths + i * tile, tile), :] = jnp.exp(-(base + state)).astype(jnp.bfloat16)
        return 0

    lax.fori_loop(0, paths // tile, walk, 0)
    rows = dates * paths
    price_rows(books, disc.at[rows:], high, low, outs[:books])
    price_rows(books, disc.at[:rows], high, low, outs[books:])


def values(here, par, kept, got, start, mats, books):
    dates, paths, width = kept.shape
    rows = dates * paths
    whole = pl.BlockSpec(memory_space=pltpu.VMEM)
    pieces = pl.pallas_call(
        functools.partial(values_kernel, books),
        in_specs=[pl.BlockSpec(memory_space=pltpu.SMEM)] + [whole] * 8,
        out_specs=[whole] * (2 * books),
        out_shape=[
            jax.ShapeDtypeStruct((rows, SETS // books), jnp.bfloat16 if i else jnp.float32)
            for i in range(books)
        ]
        * 2,
        scratch_shapes=[pltpu.VMEM((2 * rows, width), jnp.bfloat16)]
        + [pltpu.VMEM((SETS, width), jnp.bfloat16)] * 2,
        compiler_params=pltpu.CompilerParams(vmem_limit_bytes=16 * MIB),
        cost_estimate=pl.CostEstimate(
            flops=8 * rows * SETS * width, bytes_accessed=2 * MIB, transcendentals=2 * rows * width
        ),
        name="values",
    )(here, par, kept, got, start, *mats)
    return pieces[:books], pieces[books:]


def code_kernel(chips, here_ref, par_ref, kept_ref, got_ref, code_ref, group_ref, rows_ref):
    core, chip = here_ref[0], here_ref[2]
    dates, paths, _ = kept_ref.shape
    pers, vol = par_ref[0:1, :], par_ref[1:2, :]
    one = jnp.ones_like(pers)
    span = CORES * dates
    fall, block, reach = one, jnp.zeros_like(pers), 1
    for _ in range(span):
        block = block + fall
        fall = fall * pers
    inside, count = one, 0
    while reach < chips:
        bound = SHOCK * vol * block
        odd = (chip // reach) % 2 == 1
        rows_ref[4 * count : 4 * count + 1, :] = TOP / bound
        rows_ref[4 * count + 1 : 4 * count + 2, :] = jnp.where(odd, inside, 0.0) * (bound / TOP)
        rows_ref[4 * count + 2 : 4 * count + 3, :] = jnp.where(odd, one, fall)
        rows_ref[4 * count + 3 : 4 * count + 4, :] = jnp.where(odd, fall, one) * (bound / TOP)
        inside = inside * jnp.where(odd, fall, one)
        block = block + fall * block
        fall = fall * fall
        reach, count = 2 * reach, count + 1
    tile = 32
    scale = rows_ref[0:1, :]

    def walk(i, _):
        at = pl.ds(i * tile, tile)
        state = jnp.zeros((tile, pers.shape[1]), jnp.float32)
        for t in range(2 * dates):
            kept = kept_ref[t % dates, at, :].astype(jnp.float32)
            got = got_ref[t % dates, at, :].astype(jnp.float32)
            shock = jnp.where(core == 0, kept, got) if t < dates else jnp.where(core == 0, got, kept)
            state = pers * state + vol * shock
        group_ref[at, :] = state
        code_ref[at, :] = jnp.round(state * scale).astype(jnp.int16)
        return 0

    lax.fori_loop(0, paths // tile, walk, 0)


def first_code(here, par, kept, got, chips):
    dates, paths, width = kept.shape
    whole = pl.BlockSpec(memory_space=pltpu.VMEM)
    rounds = max(1, (chips - 1).bit_length())
    return pl.pallas_call(
        functools.partial(code_kernel, chips),
        in_specs=[pl.BlockSpec(memory_space=pltpu.SMEM)] + [whole] * 3,
        out_specs=[whole] * 3,
        out_shape=[
            jax.ShapeDtypeStruct((paths, width), jnp.int16),
            jax.ShapeDtypeStruct((paths, width), jnp.float32),
            jax.ShapeDtypeStruct((4 * rounds, width), jnp.float32),
        ],
        compiler_params=pltpu.CompilerParams(vmem_limit_bytes=8 * MIB),
        cost_estimate=pl.CostEstimate(
            flops=16 * paths * width, bytes_accessed=2 * MIB, transcendentals=0
        ),
        name="first_code",
    )(here, par, kept, got)


def after(array, *others):
    return lax.optimization_barrier((array,) + others)[0]


def on_device(
    shocks,
    persistence,
    volatility,
    base_rate,
    cashflows,
    block_owner,
    trade_set,
    threshold,
    margin_lag,
):
    dates, paths, width = shocks.shape
    books = lax.axis_size("book")
    chips = lax.axis_size("date") // CORES
    me = lax.axis_index("book")
    core = lax.axis_index("date") % CORES
    chip = lax.axis_index("date") // CORES
    here = jnp.stack([core, me, chip]).astype(jnp.int32)
    half = paths // CORES
    span = CORES * dates
    sets_here = SETS // books

    def side(array, which, axis):
        size = array.shape[axis] // CORES
        return lax.dynamic_slice_in_dim(array, which * size, size, axis)

    par = jnp.stack([persistence, volatility, base_rate])
    sent = side(after(shocks, par), 1 - core, 1)
    got = swap(sent)
    kept = side(after(shocks, sent), core, 1)

    code, group, table = first_code(here, par, kept, got, chips)
    start = jnp.zeros((half, width), jnp.float32)
    reach, count = 1, 0
    while reach < chips:
        scale, rate, ours, theirs = (table[4 * count + i] for i in range(4))
        if count:
            code = jnp.round(group * scale).astype(jnp.int16)
        else:
            mats = weights(after(here, code), block_owner[:, 0], trade_set, cashflows, books)
            mats_arrived = exchange(mats)
        came = across(code, reach)
        start = start + rate * came.astype(jnp.float32)
        group = ours * group + theirs * after(came, mats[0]).astype(jnp.float32)
        reach, count = 2 * reach, count + 1

    mine = after(mats[0], code)
    for arrived in mats_arrived:
        mine = mine + arrived.astype(jnp.float32)
    rounded = lax.reduce_precision(mine, 8, 7)
    high, low = rounded.astype(jnp.bfloat16), (mine - rounded).astype(jnp.bfloat16)

    late_pieces, early_pieces = values(
        here, par, kept, got, start, [high, low, swap(high), swap(low)], books
    )
    late_arrived = exchange(late_pieces)
    early_arrived = exchange(early_pieces)

    def gathered(piece, others):
        net = piece
        for arrived in others:
            net = net + arrived.astype(jnp.float32)
        return net.reshape(dates, half, sets_here)

    late_net = gathered(late_pieces[0], late_arrived)
    before = later(late_net.astype(jnp.bfloat16))
    early_net = gathered(after(early_pieces[0], late_net, before), early_arrived)
    net_got = swap(jnp.where(core == 0, late_net, early_net))
    net_kept = jnp.where(core == 0, early_net, late_net)

    joined = jnp.concatenate([before.astype(jnp.float32), early_net, late_net], 0)
    now = joined[dates:]
    collateral = jnp.zeros_like(now)
    for lag in range(1, dates + 1):
        collateral = jnp.where(
            margin_lag[None, None, :] == lag, joined[dates - lag : dates - lag + span], collateral
        )
    exposed = jnp.sum(jnp.maximum(now - collateral - threshold[None, None, :], 0.0), axis=1)
    exposed_got = swap(side(exposed, 1 - core, 0))
    net_kept = after(net_kept, exposed)
    net_value = jnp.concatenate(
        [jnp.where(core == 0, net_kept, net_got), jnp.where(core == 0, net_got, net_kept)], 1
    )
    net_value, exposed_got = lax.optimization_barrier((net_value, exposed_got))
    return (net_value, (side(exposed, core, 0) + exposed_got) / paths)


def solution(mesh):
    return jax.shard_map(
        on_device,
        mesh=mesh,
        in_specs=(
            P("date", None, "book"),
            P("book"),
            P("book"),
            P("book"),
            P("book", None),
            P("book", None),
            P("book"),
            P("book"),
            P("book"),
        ),
        out_specs=(P("date", None, "book"), P("date", "book")),
        check_vma=False,
    )
```

```python
import functools

import jax
import jax.numpy as jnp
from jax import lax
from jax.experimental import pallas as pl
from jax.experimental.pallas import tpu as pltpu
from jax.sharding import PartitionSpec as P

SETS = 512
CORES = 2
SHOCK = 6.0
TOP = 32760.0
MIB = 1 << 20
TURNED = (((1,), (1,)), ((), ()))


def swap(block):
    n = lax.axis_size("date")
    return lax.ppermute(block, "date", [(i, i ^ 1) for i in range(n)])


def across(block, chips):
    n = lax.axis_size("date")
    hop = CORES * chips
    return lax.ppermute(block, "date", [(i, i ^ hop) for i in range(n)])


def later(block):
    n = lax.axis_size("date")
    return lax.ppermute(block, "date", [(i, i + CORES) for i in range(n - CORES)])


def exchange(slots):
    n = len(slots)
    return [
        lax.ppermute(slots[i], "book", [(j, j ^ i) for j in range(n)])
        for i in range(1, n)
    ]


def weights_kernel(books, per, here_ref, owner_ref, sets_ref, flows_hbm, *refs):
    outs, total, flows, sems = refs[:books], refs[books], refs[books + 1], refs[books + 2]
    core, me = here_ref[0], here_ref[1]
    half = outs[0].shape[0]
    blocks, rows = sets_ref.shape
    sets_here = SETS // books
    size = per * rows
    copies = []
    for step in range(blocks // per):
        at = pl.ds(step * size, size)
        copies.append(pltpu.make_async_copy(flows_hbm.at[at], flows.at[at], sems.at[step]))
        copies[-1].start()
    total[...] = jnp.zeros_like(total)
    row = lax.broadcasted_iota(jnp.int32, (half, rows), 0) + core * half
    for b in range(blocks):
        if b % per == 0:
            copies[b // per].wait()
        owner = owner_ref[b]
        name = sets_ref[b : b + 1, :]
        name = ((name // sets_here) ^ owner) * sets_here + name % sets_here
        hot = jnp.where(name == row, 1.0, 0.0).astype(jnp.bfloat16)
        part = jnp.dot(
            hot, flows[b * rows : (b + 1) * rows, :], preferred_element_type=jnp.float32
        )
        slot = owner ^ me
        total[slot] = total[slot] + part
    for i in range(books):
        outs[i][...] = total[i].astype(outs[i].dtype)


def weights(here, owners, trade_set, cashflows, books):
    blocks = owners.shape[0]
    trades, width = cashflows.shape
    per = 8 if blocks % 8 == 0 else 1
    half = SETS // CORES
    whole = pl.BlockSpec(memory_space=pltpu.VMEM)
    scalars = pl.BlockSpec(memory_space=pltpu.SMEM)
    return pl.pallas_call(
        functools.partial(weights_kernel, books, per),
        in_specs=[scalars, scalars, whole, pl.BlockSpec(memory_space=pltpu.HBM)],
        out_specs=[whole] * books,
        scratch_shapes=[
            pltpu.VMEM((books, half, width), jnp.float32),
            pltpu.VMEM((trades, width), jnp.bfloat16),
            pltpu.SemaphoreType.DMA((blocks // per,)),
        ],
        out_shape=[
            jax.ShapeDtypeStruct((half, width), jnp.bfloat16 if i else jnp.float32)
            for i in range(books)
        ],
        compiler_params=pltpu.CompilerParams(vmem_limit_bytes=24 * MIB),
        cost_estimate=pl.CostEstimate(
            flops=2 * trades * half * width, bytes_accessed=2 * trades * width, transcendentals=0
        ),
        name="weights",
    )(
        here,
        pltpu.with_memory_space_constraint(owners, pltpu.HBM),
        trade_set.reshape(blocks, trades // blocks),
        pltpu.with_memory_space_constraint(cashflows, pltpu.HBM),
    )


def price_rows(books, disc, high_ref, low_ref, outs):
    sets_here = SETS // books
    rows = 256
    for r in range(disc.shape[0] // rows):
        price = disc[r * rows : (r + 1) * rows, :]
        part = lax.dot_general(price, high_ref[...], TURNED, preferred_element_type=jnp.float32)
        part = part + lax.dot_general(price, low_ref[...], TURNED, preferred_element_type=jnp.float32)
        for i in range(books):
            outs[i][r * rows : (r + 1) * rows, :] = part[:, i * sets_here : (i + 1) * sets_here].astype(
                outs[i].dtype
            )


def values_kernel(books, here_ref, par_ref, kept_ref, got_ref, start_ref, *refs):
    sources, outs, (disc, high, low) = refs[:4], refs[4:-3], refs[-3:]
    core = here_ref[0]
    dates, paths, _ = kept_ref.shape
    half = sources[0].shape[0]
    tile = 32
    for i, source in enumerate(sources):
        place = core if i < 2 else 1 - core
        target = low if i % 2 else high
        target[pl.ds(pl.multiple_of(place * half, half), half), :] = source[...]

    def walk(first, second, i, _):
        at = pl.ds(i * tile, tile)
        pers, vol, base = par_ref[0:1, :], par_ref[1:2, :], par_ref[2:3, :]
        state = start_ref[at, :]
        for t in range(2 * dates):
            source = first if t < dates else second
            state = pers * state + vol * source[t % dates, at, :].astype(jnp.float32)
            disc[pl.ds(t * paths + i * tile, tile), :] = jnp.exp(-(base + state)).astype(jnp.bfloat16)
        return 0

    @pl.when(core == 0)
    def _():
        lax.fori_loop(0, paths // tile, functools.partial(walk, kept_ref, got_ref), 0)

    @pl.when(core != 0)
    def _():
        lax.fori_loop(0, paths // tile, functools.partial(walk, got_ref, kept_ref), 0)

    rows = dates * paths
    price_rows(books, disc.at[rows:], high, low, outs[:books])
    price_rows(books, disc.at[:rows], high, low, outs[books:])


def values(here, par, kept, got, start, mats, books):
    dates, paths, width = kept.shape
    rows = dates * paths
    whole = pl.BlockSpec(memory_space=pltpu.VMEM)
    pieces = pl.pallas_call(
        functools.partial(values_kernel, books),
        in_specs=[pl.BlockSpec(memory_space=pltpu.SMEM)] + [whole] * 8,
        out_specs=[whole] * (2 * books),
        out_shape=[
            jax.ShapeDtypeStruct((rows, SETS // books), jnp.bfloat16 if i else jnp.float32)
            for i in range(books)
        ]
        * 2,
        scratch_shapes=[pltpu.VMEM((2 * rows, width), jnp.bfloat16)]
        + [pltpu.VMEM((SETS, width), jnp.bfloat16)] * 2,
        compiler_params=pltpu.CompilerParams(vmem_limit_bytes=16 * MIB),
        cost_estimate=pl.CostEstimate(
            flops=8 * rows * SETS * width, bytes_accessed=2 * MIB, transcendentals=2 * rows * width
        ),
        name="values",
    )(here, par, kept, got, start, *mats)
    return pieces[:books], pieces[books:]


def code_kernel(chips, here_ref, par_ref, kept_ref, got_ref, code_ref, group_ref, rows_ref):
    core, chip = here_ref[0], here_ref[2]
    dates, paths, _ = kept_ref.shape
    pers, vol = par_ref[0:1, :], par_ref[1:2, :]
    one = jnp.ones_like(pers)
    span = CORES * dates
    fall, block, reach = one, jnp.zeros_like(pers), 1
    for _ in range(span):
        block = block + fall
        fall = fall * pers
    inside, count = one, 0
    while reach < chips:
        bound = SHOCK * vol * block
        odd = (chip // reach) % 2 == 1
        rows_ref[4 * count : 4 * count + 1, :] = TOP / bound
        rows_ref[4 * count + 1 : 4 * count + 2, :] = jnp.where(odd, inside, 0.0) * (bound / TOP)
        rows_ref[4 * count + 2 : 4 * count + 3, :] = jnp.where(odd, one, fall)
        rows_ref[4 * count + 3 : 4 * count + 4, :] = jnp.where(odd, fall, one) * (bound / TOP)
        inside = inside * jnp.where(odd, fall, one)
        block = block + fall * block
        fall = fall * fall
        reach, count = 2 * reach, count + 1
    tile = 32
    scale = rows_ref[0:1, :]

    def walk(first, second, i, _):
        at = pl.ds(i * tile, tile)
        state = jnp.zeros((tile, pers.shape[1]), jnp.float32)
        for t in range(2 * dates):
            source = first if t < dates else second
            state = pers * state + source[t % dates, at, :].astype(jnp.float32)
        state = vol * state
        group_ref[at, :] = state
        code_ref[at, :] = jnp.round(state * scale).astype(jnp.int16)
        return 0

    @pl.when(core == 0)
    def _():
        lax.fori_loop(0, paths // tile, functools.partial(walk, kept_ref, got_ref), 0)

    @pl.when(core != 0)
    def _():
        lax.fori_loop(0, paths // tile, functools.partial(walk, got_ref, kept_ref), 0)


def first_code(here, par, kept, got, chips):
    dates, paths, width = kept.shape
    whole = pl.BlockSpec(memory_space=pltpu.VMEM)
    rounds = max(1, (chips - 1).bit_length())
    return pl.pallas_call(
        functools.partial(code_kernel, chips),
        in_specs=[pl.BlockSpec(memory_space=pltpu.SMEM)] + [whole] * 3,
        out_specs=[whole] * 3,
        out_shape=[
            jax.ShapeDtypeStruct((paths, width), jnp.int16),
            jax.ShapeDtypeStruct((paths, width), jnp.float32),
            jax.ShapeDtypeStruct((4 * rounds, width), jnp.float32),
        ],
        compiler_params=pltpu.CompilerParams(vmem_limit_bytes=8 * MIB),
        cost_estimate=pl.CostEstimate(
            flops=16 * paths * width, bytes_accessed=2 * MIB, transcendentals=0
        ),
        name="first_code",
    )(here, par, kept, got)


def after(array, *others):
    return lax.optimization_barrier((array,) + others)[0]


def on_device(
    shocks,
    persistence,
    volatility,
    base_rate,
    cashflows,
    block_owner,
    trade_set,
    threshold,
    margin_lag,
):
    dates, paths, width = shocks.shape
    books = lax.axis_size("book")
    chips = lax.axis_size("date") // CORES
    me = lax.axis_index("book")
    core = lax.axis_index("date") % CORES
    chip = lax.axis_index("date") // CORES
    here = jnp.stack([core, me, chip]).astype(jnp.int32)
    half = paths // CORES
    span = CORES * dates
    sets_here = SETS // books

    def side(array, which, axis):
        size = array.shape[axis] // CORES
        return lax.dynamic_slice_in_dim(array, which * size, size, axis)

    par = jnp.stack([persistence, volatility, base_rate])
    sent = side(after(shocks, par), 1 - core, 1)
    got = swap(sent)
    kept = side(after(shocks, sent), core, 1)

    code, group, table = first_code(here, par, kept, got, chips)
    start = jnp.zeros((half, width), jnp.float32)
    reach, count = 1, 0
    while reach < chips:
        scale, rate, ours, theirs = (table[4 * count + i] for i in range(4))
        if count:
            code = jnp.round(group * scale).astype(jnp.int16)
        else:
            mats = weights(after(here, code), block_owner[:, 0], trade_set, cashflows, books)
            mats_arrived = exchange(mats)
        came = across(code, reach)
        start = start + rate * came.astype(jnp.float32)
        group = ours * group + theirs * after(came, mats[0]).astype(jnp.float32)
        reach, count = 2 * reach, count + 1

    kept = side(after(shocks, code), core, 1)
    mine = after(mats[0], code)
    for arrived in mats_arrived:
        mine = mine + arrived.astype(jnp.float32)
    rounded = lax.reduce_precision(mine, 8, 7)
    high, low = rounded.astype(jnp.bfloat16), (mine - rounded).astype(jnp.bfloat16)

    late_pieces, early_pieces = values(
        here, par, kept, got, start, [high, low, swap(high), swap(low)], books
    )
    late_arrived = exchange(late_pieces)
    early_arrived = exchange(early_pieces)

    def gathered(piece, others):
        net = piece
        for arrived in others:
            net = net + arrived.astype(jnp.float32)
        return net.reshape(dates, half, sets_here)

    late_net = gathered(late_pieces[0], late_arrived)
    before = later(late_net.astype(jnp.bfloat16))
    early_net = gathered(after(early_pieces[0], late_net), early_arrived)
    net_got = swap(jnp.where(core == 0, late_net, early_net))
    net_kept = jnp.where(core == 0, early_net, late_net)

    joined = jnp.concatenate([before.astype(jnp.float32), early_net, late_net], 0)
    now = joined[dates:]
    collateral = jnp.zeros_like(now)
    for lag in range(1, dates + 1):
        collateral = jnp.where(
            margin_lag[None, None, :] == lag, joined[dates - lag : dates - lag + span], collateral
        )
    exposed = jnp.sum(jnp.maximum(now - collateral - threshold[None, None, :], 0.0), axis=1)
    exposed_got = swap(side(exposed, 1 - core, 0))
    net_value = jnp.concatenate(
        [jnp.where(core == 0, net_kept, net_got), jnp.where(core == 0, net_got, net_kept)], 1
    )
    net_value, exposed_got = lax.optimization_barrier((net_value, exposed_got))
    return (net_value, (side(exposed, core, 0) + exposed_got) / paths)


def solution(mesh):
    return jax.shard_map(
        on_device,
        mesh=mesh,
        in_specs=(
            P("date", None, "book"),
            P("book"),
            P("book"),
            P("book"),
            P("book", None),
            P("book", None),
            P("book"),
            P("book"),
            P("book"),
        ),
        out_specs=(P("date", None, "book"), P("date", "book")),
        check_vma=False,
    )
```

```python
import functools

import jax
import jax.numpy as jnp
from jax import lax
from jax.experimental import pallas as pl
from jax.experimental.pallas import tpu as pltpu
from jax.sharding import PartitionSpec as P

SETS = 512
CORES = 2
SHOCK = 6.0
TOP = 32760.0
MIB = 1 << 20
TURNED = (((1,), (1,)), ((), ()))


def swap(block):
    n = lax.axis_size("date")
    return lax.ppermute(block, "date", [(i, i ^ 1) for i in range(n)])


def across(block, chips):
    n = lax.axis_size("date")
    hop = CORES * chips
    return lax.ppermute(block, "date", [(i, i ^ hop) for i in range(n)])


def later(block):
    n = lax.axis_size("date")
    return lax.ppermute(block, "date", [(i, i + CORES) for i in range(n - CORES)])


def exchange(slots):
    n = len(slots)
    return [
        lax.ppermute(slots[i], "book", [(j, j ^ i) for j in range(n)])
        for i in range(1, n)
    ]


def weights_kernel(books, per, here_ref, owner_ref, sets_ref, flows_hbm, *refs):
    outs, total, flows, sems = refs[:books], refs[books], refs[books + 1], refs[books + 2]
    core, me = here_ref[0], here_ref[1]
    half = outs[0].shape[0]
    blocks, rows = sets_ref.shape
    sets_here = SETS // books
    size = per * rows
    copies = []
    for step in range(blocks // per):
        at = pl.ds(step * size, size)
        copies.append(pltpu.make_async_copy(flows_hbm.at[at], flows.at[at], sems.at[step]))
        copies[-1].start()
    total[...] = jnp.zeros_like(total)
    row = lax.broadcasted_iota(jnp.int32, (half, rows), 0) + core * half
    for b in range(blocks):
        if b % per == 0:
            copies[b // per].wait()
        owner = owner_ref[b]
        name = sets_ref[b : b + 1, :]
        name = ((name // sets_here) ^ owner) * sets_here + name % sets_here
        hot = jnp.where(name == row, 1.0, 0.0).astype(jnp.bfloat16)
        part = jnp.dot(
            hot, flows[b * rows : (b + 1) * rows, :], preferred_element_type=jnp.float32
        )
        slot = owner ^ me
        total[slot] = total[slot] + part
    for i in range(books):
        outs[i][...] = total[i].astype(outs[i].dtype)


def weights(here, owners, trade_set, cashflows, books):
    blocks = owners.shape[0]
    trades, width = cashflows.shape
    per = 8 if blocks % 8 == 0 else 1
    half = SETS // CORES
    whole = pl.BlockSpec(memory_space=pltpu.VMEM)
    scalars = pl.BlockSpec(memory_space=pltpu.SMEM)
    return pl.pallas_call(
        functools.partial(weights_kernel, books, per),
        in_specs=[scalars, scalars, whole, pl.BlockSpec(memory_space=pltpu.HBM)],
        out_specs=[whole] * books,
        scratch_shapes=[
            pltpu.VMEM((books, half, width), jnp.float32),
            pltpu.VMEM((trades, width), jnp.bfloat16),
            pltpu.SemaphoreType.DMA((blocks // per,)),
        ],
        out_shape=[
            jax.ShapeDtypeStruct((half, width), jnp.bfloat16 if i else jnp.float32)
            for i in range(books)
        ],
        compiler_params=pltpu.CompilerParams(vmem_limit_bytes=24 * MIB),
        cost_estimate=pl.CostEstimate(
            flops=2 * trades * half * width, bytes_accessed=2 * trades * width, transcendentals=0
        ),
        name="weights",
    )(
        here,
        pltpu.with_memory_space_constraint(owners, pltpu.HBM),
        trade_set.reshape(blocks, trades // blocks),
        pltpu.with_memory_space_constraint(cashflows, pltpu.HBM),
    )


def price_rows(books, disc, high_ref, low_ref, outs):
    sets_here = SETS // books
    rows = 256
    for r in range(disc.shape[0] // rows):
        price = disc[r * rows : (r + 1) * rows, :]
        part = lax.dot_general(price, high_ref[...], TURNED, preferred_element_type=jnp.float32)
        part = part + lax.dot_general(price, low_ref[...], TURNED, preferred_element_type=jnp.float32)
        for i in range(books):
            outs[i][r * rows : (r + 1) * rows, :] = part[:, i * sets_here : (i + 1) * sets_here].astype(
                outs[i].dtype
            )


def values_kernel(books, here_ref, par_ref, kept_ref, got_ref, start_ref, *refs):
    sources, outs, (disc, high, low) = refs[:4], refs[4:-3], refs[-3:]
    core = here_ref[0]
    dates, paths, _ = kept_ref.shape
    half = sources[0].shape[0]
    tile = 32
    for i, source in enumerate(sources):
        place = core if i < 2 else 1 - core
        target = low if i % 2 else high
        target[pl.ds(pl.multiple_of(place * half, half), half), :] = source[...]

    def walk(first, second, i, _):
        at = pl.ds(i * tile, tile)
        pers, vol, base = par_ref[0:1, :], par_ref[1:2, :], par_ref[2:3, :]
        state = start_ref[at, :]
        for t in range(2 * dates):
            source = first if t < dates else second
            state = pers * state + vol * source[t % dates, at, :].astype(jnp.float32)
            disc[pl.ds(t * paths + i * tile, tile), :] = jnp.exp(-(base + state)).astype(jnp.bfloat16)
        return 0

    @pl.when(core == 0)
    def _():
        lax.fori_loop(0, paths // tile, functools.partial(walk, kept_ref, got_ref), 0)

    @pl.when(core != 0)
    def _():
        lax.fori_loop(0, paths // tile, functools.partial(walk, got_ref, kept_ref), 0)

    rows = dates * paths
    price_rows(books, disc.at[rows:], high, low, outs[:books])
    price_rows(books, disc.at[:rows], high, low, outs[books:])


def values(here, par, kept, got, start, mats, books):
    dates, paths, width = kept.shape
    rows = dates * paths
    whole = pl.BlockSpec(memory_space=pltpu.VMEM)
    pieces = pl.pallas_call(
        functools.partial(values_kernel, books),
        in_specs=[pl.BlockSpec(memory_space=pltpu.SMEM)] + [whole] * 8,
        out_specs=[whole] * (2 * books),
        out_shape=[
            jax.ShapeDtypeStruct((rows, SETS // books), jnp.bfloat16 if i else jnp.float32)
            for i in range(books)
        ]
        * 2,
        scratch_shapes=[pltpu.VMEM((2 * rows, width), jnp.bfloat16)]
        + [pltpu.VMEM((SETS, width), jnp.bfloat16)] * 2,
        compiler_params=pltpu.CompilerParams(vmem_limit_bytes=16 * MIB),
        cost_estimate=pl.CostEstimate(
            flops=8 * rows * SETS * width, bytes_accessed=2 * MIB, transcendentals=2 * rows * width
        ),
        name="values",
    )(here, par, kept, got, start, *mats)
    return pieces[:books], pieces[books:]


def code_kernel(chips, here_ref, par_ref, kept_ref, got_ref, code_ref, group_ref, rows_ref):
    core, chip = here_ref[0], here_ref[2]
    dates, paths, _ = kept_ref.shape
    pers, vol = par_ref[0:1, :], par_ref[1:2, :]
    one = jnp.ones_like(pers)
    span = CORES * dates
    fall, block, reach = one, jnp.zeros_like(pers), 1
    for _ in range(span):
        block = block + fall
        fall = fall * pers
    inside, count = one, 0
    while reach < chips:
        bound = SHOCK * vol * block
        odd = (chip // reach) % 2 == 1
        rows_ref[4 * count : 4 * count + 1, :] = TOP / bound
        rows_ref[4 * count + 1 : 4 * count + 2, :] = jnp.where(odd, inside, 0.0) * (bound / TOP)
        rows_ref[4 * count + 2 : 4 * count + 3, :] = jnp.where(odd, one, fall)
        rows_ref[4 * count + 3 : 4 * count + 4, :] = jnp.where(odd, fall, one) * (bound / TOP)
        inside = inside * jnp.where(odd, fall, one)
        block = block + fall * block
        fall = fall * fall
        reach, count = 2 * reach, count + 1
    tile = 32
    scale = rows_ref[0:1, :]

    def walk(first, second, i, _):
        at = pl.ds(i * tile, tile)
        state = jnp.zeros((tile, pers.shape[1]), jnp.float32)
        for t in range(2 * dates):
            source = first if t < dates else second
            state = pers * state + source[t % dates, at, :].astype(jnp.float32)
        state = vol * state
        group_ref[at, :] = state
        code_ref[at, :] = jnp.round(state * scale).astype(jnp.int16)
        return 0

    @pl.when(core == 0)
    def _():
        lax.fori_loop(0, paths // tile, functools.partial(walk, kept_ref, got_ref), 0)

    @pl.when(core != 0)
    def _():
        lax.fori_loop(0, paths // tile, functools.partial(walk, got_ref, kept_ref), 0)


def first_code(here, par, kept, got, chips):
    dates, paths, width = kept.shape
    whole = pl.BlockSpec(memory_space=pltpu.VMEM)
    rounds = max(1, (chips - 1).bit_length())
    return pl.pallas_call(
        functools.partial(code_kernel, chips),
        in_specs=[pl.BlockSpec(memory_space=pltpu.SMEM)] + [whole] * 3,
        out_specs=[whole] * 3,
        out_shape=[
            jax.ShapeDtypeStruct((paths, width), jnp.int16),
            jax.ShapeDtypeStruct((paths, width), jnp.float32),
            jax.ShapeDtypeStruct((4 * rounds, width), jnp.float32),
        ],
        compiler_params=pltpu.CompilerParams(vmem_limit_bytes=8 * MIB),
        cost_estimate=pl.CostEstimate(
            flops=16 * paths * width, bytes_accessed=2 * MIB, transcendentals=0
        ),
        name="first_code",
    )(here, par, kept, got)


def after(array, *others):
    return lax.optimization_barrier((array,) + others)[0]


def on_device(
    shocks,
    persistence,
    volatility,
    base_rate,
    cashflows,
    block_owner,
    trade_set,
    threshold,
    margin_lag,
):
    dates, paths, width = shocks.shape
    books = lax.axis_size("book")
    chips = lax.axis_size("date") // CORES
    me = lax.axis_index("book")
    core = lax.axis_index("date") % CORES
    chip = lax.axis_index("date") // CORES
    here = jnp.stack([core, me, chip]).astype(jnp.int32)
    half = paths // CORES
    span = CORES * dates
    sets_here = SETS // books

    def side(array, which, axis):
        size = array.shape[axis] // CORES
        return lax.dynamic_slice_in_dim(array, which * size, size, axis)

    sent = side(shocks, 1 - core, 1)
    par = jnp.stack([persistence, volatility, after(base_rate, sent)])
    got = swap(sent)
    kept = side(after(shocks, sent), core, 1)

    code, group, table = first_code(here, par, kept, got, chips)
    start = jnp.zeros((half, width), jnp.float32)
    reach, count = 1, 0
    while reach < chips:
        scale, rate, ours, theirs = (table[4 * count + i] for i in range(4))
        if count:
            code = jnp.round(group * scale).astype(jnp.int16)
        else:
            mats = weights(after(here, code), block_owner[:, 0], trade_set, cashflows, books)
            mats_arrived = exchange(mats)
        came = across(code, reach)
        start = start + rate * came.astype(jnp.float32)
        group = ours * group + theirs * after(came, mats[0]).astype(jnp.float32)
        reach, count = 2 * reach, count + 1

    kept = side(after(shocks, code), core, 1)
    mine = after(mats[0], code)
    for arrived in mats_arrived:
        mine = mine + arrived.astype(jnp.float32)
    rounded = lax.reduce_precision(mine, 8, 7)
    high, low = rounded.astype(jnp.bfloat16), (mine - rounded).astype(jnp.bfloat16)

    late_pieces, early_pieces = values(
        here, par, kept, got, start, [high, low, swap(high), swap(low)], books
    )
    late_arrived = exchange(late_pieces)
    early_arrived = exchange(early_pieces)

    def gathered(piece, others):
        net = piece
        for arrived in others:
            net = net + arrived.astype(jnp.float32)
        return net.reshape(dates, half, sets_here)

    late_net = gathered(late_pieces[0], late_arrived)
    before = later(late_net.astype(jnp.bfloat16))
    early_net = gathered(after(early_pieces[0], late_net), early_arrived)
    net_got = swap(jnp.where(core == 0, late_net, early_net))
    net_kept = jnp.where(core == 0, early_net, late_net)

    joined = jnp.concatenate([before.astype(jnp.float32), early_net, late_net], 0)
    now = joined[dates:]
    collateral = jnp.zeros_like(now)
    for lag in range(1, dates + 1):
        collateral = jnp.where(
            margin_lag[None, None, :] == lag, joined[dates - lag : dates - lag + span], collateral
        )
    exposed = jnp.sum(jnp.maximum(now - collateral - threshold[None, None, :], 0.0), axis=1)
    exposed_got = swap(side(exposed, 1 - core, 0))
    net_value = jnp.concatenate(
        [jnp.where(core == 0, net_kept, net_got), jnp.where(core == 0, net_got, net_kept)], 1
    )
    net_value, exposed_got = lax.optimization_barrier((net_value, exposed_got))
    return (net_value, (side(exposed, core, 0) + exposed_got) / paths)


def solution(mesh):
    return jax.shard_map(
        on_device,
        mesh=mesh,
        in_specs=(
            P("date", None, "book"),
            P("book"),
            P("book"),
            P("book"),
            P("book", None),
            P("book", None),
            P("book"),
            P("book"),
            P("book"),
        ),
        out_specs=(P("date", None, "book"), P("date", "book")),
        check_vma=False,
    )
```

```python
import functools

import jax
import jax.numpy as jnp
from jax import lax
from jax.experimental import pallas as pl
from jax.experimental.pallas import tpu as pltpu
from jax.sharding import PartitionSpec as P

SETS = 512
CORES = 2
SHOCK = 6.0
TOP = 32760.0
MIB = 1 << 20
TURNED = (((1,), (1,)), ((), ()))


def swap(block):
    n = lax.axis_size("date")
    return lax.ppermute(block, "date", [(i, i ^ 1) for i in range(n)])


def across(block, chips):
    n = lax.axis_size("date")
    hop = CORES * chips
    return lax.ppermute(block, "date", [(i, i ^ hop) for i in range(n)])


def later(block):
    n = lax.axis_size("date")
    return lax.ppermute(block, "date", [(i, i + CORES) for i in range(n - CORES)])


def exchange(slots):
    n = len(slots)
    return [
        lax.ppermute(slots[i], "book", [(j, j ^ i) for j in range(n)])
        for i in range(1, n)
    ]


def weights_kernel(books, per, here_ref, owner_ref, sets_ref, flows_hbm, *refs):
    outs, total, flows, sems = refs[:books], refs[books], refs[books + 1], refs[books + 2]
    core, me = here_ref[0], here_ref[1]
    half = outs[0].shape[0]
    blocks, rows = sets_ref.shape
    sets_here = SETS // books
    size = per * rows
    copies = []
    for step in range(blocks // per):
        at = pl.ds(step * size, size)
        copies.append(pltpu.make_async_copy(flows_hbm.at[at], flows.at[at], sems.at[step]))
        copies[-1].start()
    total[...] = jnp.zeros_like(total)
    row = lax.broadcasted_iota(jnp.int32, (half, rows), 0) + core * half
    for b in range(blocks):
        if b % per == 0:
            copies[b // per].wait()
        owner = owner_ref[b]
        name = sets_ref[b : b + 1, :]
        name = ((name // sets_here) ^ owner) * sets_here + name % sets_here
        hot = jnp.where(name == row, 1.0, 0.0).astype(jnp.bfloat16)
        part = jnp.dot(
            hot, flows[b * rows : (b + 1) * rows, :], preferred_element_type=jnp.float32
        )
        slot = owner ^ me
        total[slot] = total[slot] + part
    for i in range(books):
        outs[i][...] = total[i].astype(outs[i].dtype)


def weights(here, owners, trade_set, cashflows, books):
    blocks = owners.shape[0]
    trades, width = cashflows.shape
    per = 8 if blocks % 8 == 0 else 1
    half = SETS // CORES
    whole = pl.BlockSpec(memory_space=pltpu.VMEM)
    scalars = pl.BlockSpec(memory_space=pltpu.SMEM)
    return pl.pallas_call(
        functools.partial(weights_kernel, books, per),
        in_specs=[scalars, scalars, whole, pl.BlockSpec(memory_space=pltpu.HBM)],
        out_specs=[whole] * books,
        scratch_shapes=[
            pltpu.VMEM((books, half, width), jnp.float32),
            pltpu.VMEM((trades, width), jnp.bfloat16),
            pltpu.SemaphoreType.DMA((blocks // per,)),
        ],
        out_shape=[
            jax.ShapeDtypeStruct((half, width), jnp.bfloat16 if i else jnp.float32)
            for i in range(books)
        ],
        compiler_params=pltpu.CompilerParams(vmem_limit_bytes=24 * MIB),
        cost_estimate=pl.CostEstimate(
            flops=2 * trades * half * width, bytes_accessed=2 * trades * width, transcendentals=0
        ),
        name="weights",
    )(
        here,
        pltpu.with_memory_space_constraint(owners, pltpu.HBM),
        trade_set.reshape(blocks, trades // blocks),
        pltpu.with_memory_space_constraint(cashflows, pltpu.HBM),
    )


def price_rows(books, core, disc, sources, outs):
    sets_here = SETS // books
    half = sources[0].shape[0]
    rows = 256

    def product(price, high, low):
        part = lax.dot_general(price, high[...], TURNED, preferred_element_type=jnp.float32)
        return part + lax.dot_general(price, low[...], TURNED, preferred_element_type=jnp.float32)

    for r in range(disc.shape[0] // rows):
        price = disc[r * rows : (r + 1) * rows, :]
        mine, other = product(price, *sources[:2]), product(price, *sources[2:])
        sides = jnp.where(core == 0, mine, other), jnp.where(core == 0, other, mine)
        for i in range(books):
            which, at = divmod(i * sets_here, half)
            outs[i][r * rows : (r + 1) * rows, :] = sides[which][:, at : at + sets_here].astype(outs[i].dtype)


def values_kernel(books, here_ref, par_ref, kept_ref, got_ref, start_ref, *refs):
    sources, outs, disc = refs[:4], refs[4:-1], refs[-1]
    core = here_ref[0]
    dates, paths, _ = kept_ref.shape
    tile = 32

    def walk(first, second, i, _):
        at = pl.ds(i * tile, tile)
        pers, vol, base = par_ref[0:1, :], par_ref[1:2, :], par_ref[2:3, :]
        state = start_ref[at, :]
        for t in range(2 * dates):
            source = first if t < dates else second
            state = pers * state + vol * source[t % dates, at, :].astype(jnp.float32)
            disc[pl.ds(t * paths + i * tile, tile), :] = jnp.exp(-(base + state)).astype(jnp.bfloat16)
        return 0

    @pl.when(core == 0)
    def _():
        lax.fori_loop(0, paths // tile, functools.partial(walk, kept_ref, got_ref), 0)

    @pl.when(core != 0)
    def _():
        lax.fori_loop(0, paths // tile, functools.partial(walk, got_ref, kept_ref), 0)

    rows = dates * paths
    price_rows(books, core, disc.at[rows:], sources, outs[:books])
    price_rows(books, core, disc.at[:rows], sources, outs[books:])


def values(here, par, kept, got, start, mats, books):
    dates, paths, width = kept.shape
    rows = dates * paths
    whole = pl.BlockSpec(memory_space=pltpu.VMEM)
    pieces = pl.pallas_call(
        functools.partial(values_kernel, books),
        in_specs=[pl.BlockSpec(memory_space=pltpu.SMEM)] + [whole] * 8,
        out_specs=[whole] * (2 * books),
        out_shape=[
            jax.ShapeDtypeStruct((rows, SETS // books), jnp.bfloat16 if i else jnp.float32)
            for i in range(books)
        ]
        * 2,
        scratch_shapes=[pltpu.VMEM((2 * rows, width), jnp.bfloat16)],
        compiler_params=pltpu.CompilerParams(vmem_limit_bytes=16 * MIB),
        cost_estimate=pl.CostEstimate(
            flops=8 * rows * SETS * width, bytes_accessed=2 * MIB, transcendentals=2 * rows * width
        ),
        name="values",
    )(here, par, kept, got, start, *mats)
    return pieces[:books], pieces[books:]


def code_kernel(chips, here_ref, par_ref, kept_ref, got_ref, code_ref, group_ref, rows_ref):
    core, chip = here_ref[0], here_ref[2]
    dates, paths, _ = kept_ref.shape
    pers, vol = par_ref[0:1, :], par_ref[1:2, :]
    one = jnp.ones_like(pers)
    span = CORES * dates
    fall, block, reach = one, jnp.zeros_like(pers), 1
    for _ in range(span):
        block = block + fall
        fall = fall * pers
    inside, count = one, 0
    while reach < chips:
        bound = SHOCK * vol * block
        odd = (chip // reach) % 2 == 1
        rows_ref[4 * count : 4 * count + 1, :] = TOP / bound
        rows_ref[4 * count + 1 : 4 * count + 2, :] = jnp.where(odd, inside, 0.0) * (bound / TOP)
        rows_ref[4 * count + 2 : 4 * count + 3, :] = jnp.where(odd, one, fall)
        rows_ref[4 * count + 3 : 4 * count + 4, :] = jnp.where(odd, fall, one) * (bound / TOP)
        inside = inside * jnp.where(odd, fall, one)
        block = block + fall * block
        fall = fall * fall
        reach, count = 2 * reach, count + 1
    tile = 32
    scale = rows_ref[0:1, :]

    def walk(first, second, i, _):
        at = pl.ds(i * tile, tile)
        state = jnp.zeros((tile, pers.shape[1]), jnp.float32)
        for t in range(2 * dates):
            source = first if t < dates else second
            state = pers * state + source[t % dates, at, :].astype(jnp.float32)
        state = vol * state
        group_ref[at, :] = state
        code_ref[at, :] = jnp.round(state * scale).astype(jnp.int16)
        return 0

    @pl.when(core == 0)
    def _():
        lax.fori_loop(0, paths // tile, functools.partial(walk, kept_ref, got_ref), 0)

    @pl.when(core != 0)
    def _():
        lax.fori_loop(0, paths // tile, functools.partial(walk, got_ref, kept_ref), 0)


def first_code(here, par, kept, got, chips):
    dates, paths, width = kept.shape
    whole = pl.BlockSpec(memory_space=pltpu.VMEM)
    rounds = max(1, (chips - 1).bit_length())
    return pl.pallas_call(
        functools.partial(code_kernel, chips),
        in_specs=[pl.BlockSpec(memory_space=pltpu.SMEM)] + [whole] * 3,
        out_specs=[whole] * 3,
        out_shape=[
            jax.ShapeDtypeStruct((paths, width), jnp.int16),
            jax.ShapeDtypeStruct((paths, width), jnp.float32),
            jax.ShapeDtypeStruct((4 * rounds, width), jnp.float32),
        ],
        compiler_params=pltpu.CompilerParams(vmem_limit_bytes=8 * MIB),
        cost_estimate=pl.CostEstimate(
            flops=16 * paths * width, bytes_accessed=2 * MIB, transcendentals=0
        ),
        name="first_code",
    )(here, par, kept, got)


def after(array, *others):
    return lax.optimization_barrier((array,) + others)[0]


def on_device(
    shocks,
    persistence,
    volatility,
    base_rate,
    cashflows,
    block_owner,
    trade_set,
    threshold,
    margin_lag,
):
    dates, paths, width = shocks.shape
    books = lax.axis_size("book")
    chips = lax.axis_size("date") // CORES
    me = lax.axis_index("book")
    core = lax.axis_index("date") % CORES
    chip = lax.axis_index("date") // CORES
    here = jnp.stack([core, me, chip]).astype(jnp.int32)
    half = paths // CORES
    span = CORES * dates
    sets_here = SETS // books

    def side(array, which, axis):
        size = array.shape[axis] // CORES
        return lax.dynamic_slice_in_dim(array, which * size, size, axis)

    par = jnp.stack([persistence, volatility, base_rate])
    sent = side(after(shocks, par), 1 - core, 1)
    got = swap(sent)
    kept = side(after(shocks, sent), core, 1)

    code, group, table = first_code(here, par, kept, got, chips)
    start = jnp.zeros((half, width), jnp.float32)
    reach, count = 1, 0
    while reach < chips:
        scale, rate, ours, theirs = (table[4 * count + i] for i in range(4))
        if count:
            code = jnp.round(group * scale).astype(jnp.int16)
        else:
            mats = weights(after(here, code), block_owner[:, 0], trade_set, cashflows, books)
            mats_arrived = exchange(mats)
        came = across(code, reach)
        start = start + rate * came.astype(jnp.float32)
        group = ours * group + theirs * after(came, mats[0]).astype(jnp.float32)
        reach, count = 2 * reach, count + 1

    kept = side(after(shocks, code), core, 1)
    mine = after(mats[0], code)
    for arrived in mats_arrived:
        mine = mine + arrived.astype(jnp.float32)
    rounded = lax.reduce_precision(mine, 8, 7)
    high, low = rounded.astype(jnp.bfloat16), (mine - rounded).astype(jnp.bfloat16)

    late_pieces, early_pieces = values(
        here, par, kept, got, start, [high, low, swap(high), swap(low)], books
    )
    late_arrived = exchange(late_pieces)
    early_arrived = exchange(early_pieces)

    def gathered(piece, others):
        net = piece
        for arrived in others:
            net = net + arrived.astype(jnp.float32)
        return net.reshape(dates, half, sets_here)

    late_net = gathered(late_pieces[0], late_arrived)
    before = later(late_net.astype(jnp.bfloat16))
    early_net = gathered(after(early_pieces[0], late_net), early_arrived)
    net_got = swap(jnp.where(core == 0, late_net, early_net))
    net_kept = jnp.where(core == 0, early_net, late_net)

    joined = jnp.concatenate([before.astype(jnp.float32), early_net, late_net], 0)
    now = joined[dates:]
    collateral = jnp.zeros_like(now)
    for lag in range(1, dates + 1):
        collateral = jnp.where(
            margin_lag[None, None, :] == lag, joined[dates - lag : dates - lag + span], collateral
        )
    exposed = jnp.sum(jnp.maximum(now - collateral - threshold[None, None, :], 0.0), axis=1)
    exposed_got = swap(side(exposed, 1 - core, 0))
    net_value = jnp.concatenate(
        [jnp.where(core == 0, net_kept, net_got), jnp.where(core == 0, net_got, net_kept)], 1
    )
    net_value, exposed_got = lax.optimization_barrier((net_value, exposed_got))
    return (net_value, (side(exposed, core, 0) + exposed_got) / paths)


def solution(mesh):
    return jax.shard_map(
        on_device,
        mesh=mesh,
        in_specs=(
            P("date", None, "book"),
            P("book"),
            P("book"),
            P("book"),
            P("book", None),
            P("book", None),
            P("book"),
            P("book"),
            P("book"),
        ),
        out_specs=(P("date", None, "book"), P("date", "book")),
        check_vma=False,
    )
```
